128 devices in a mesh: seg: 8 (over x, core), row: 16 (over y, z).
Axes of the slice: x: 4, y: 4, z: 4, core: 2. Of those that a mesh axis runs over, the one named last changes fastest.
Arguments:
- terminal_adjoint: float32 [8, 2, 2048, 2048], P('seg', None, 'row'), may hold values from -6 to 6
- midpoint_state: float32 [8, 1, 2, 2048, 2048], P('seg', None, None, 'row'), may hold values from -6 to 6
- controls: float32 [8, 1, 4], P('seg'), may hold values from -8 to 8
- detuning: float32 [4], replicated, may hold values from -3 to 3
- anharmonicity: float32 [4], replicated, may hold values from 0.2 to 1
- decay_rate: float32 [4], replicated, may hold values from 0.2 to 2
- dephasing: float32 [4], replicated, may hold values from 0.1 to 1
- cross_kerr: float32 [6], replicated, may hold values from 0.05 to 0.3
Outputs:
- start_adjoint: float32 [8, 2, 2048, 2048], P('seg', None, 'row')
- continuity_defect: float32 [8, 2, 2048, 2048], P('seg', None, 'row')
- control_gradient: float32 [8, 1, 4], P('seg')
The draws below stay inside these ranges and needn't reach their ends.
All inputs are finite; a program needn't handle non-finite values.
Results may differ from the reference program's by a relative error of at most 0.00011.
Values sent between devices are 32-bit elements; how exact they have to be, the bound alone decides.
No kernel may reach another device: no remote copies, remote signals or barrier semaphores. Data moves between devices by JAX's collectives and lax.ppermute only.
A program may use at most 128 MiB of HBM per device.

```python
import math
import jax
import jax.numpy as jnp
import numpy as np
from jax import lax

LEVELS = 8
LAST_LEVELS = 4
QUDITS = 4
STEPS = 1
SWEEPS = 2
PAIRS = 6
ORDER = 2048
SEGMENTS = 8


def shard_levels(stream_key, dims, split, low, top_value):
    factor_of = 1.0
    for axis_at, blocks in split:
        heights = jax.random.uniform(jax.random.fold_in(jax.random.fold_in(stream_key, 6), axis_at), (blocks,), jnp.float32, low / len(split), top_value / len(split))
        factor_of = factor_of * jnp.repeat(jnp.exp(heights), dims[axis_at] // blocks).reshape((-1,) + (1,) * (len(dims) - 1 - axis_at))
    return factor_of


def normal_values(key, dims, scale, reach, split=(), kind=jnp.bfloat16):
    gain = shard_levels(key, dims, split, -0.22, 0.18) if split else 1.0
    array = jax.random.normal(key, dims, jnp.float32) * scale * gain
    return jnp.minimum(jnp.maximum(array, -reach), reach).astype(kind)


def setup_inputs(seed: int = 0) -> dict:
    key_of = jax.random.split(jax.random.key(seed), 9)
    return {
        "terminal_adjoint": normal_values(key_of[0], (SEGMENTS, 2, ORDER, ORDER), 1.0, 6.0, ((0, 8), (2, 16)), jnp.float32),
        "midpoint_state": normal_values(key_of[1], (SEGMENTS, STEPS, 2, ORDER, ORDER), 1.0, 6.0, ((0, 8), (3, 16)), jnp.float32),
        "controls": normal_values(key_of[2], (SEGMENTS, STEPS, QUDITS), 2.0, 8.0, ((0, 8),), jnp.float32),
        "detuning": jnp.clip(jax.random.uniform(key_of[3], (QUDITS,), jnp.float32, -3.0, 3.0), -3.0, 3.0),
        "anharmonicity": jnp.clip(jnp.exp(jax.random.uniform(key_of[4], (QUDITS,), jnp.float32, math.log(0.2), math.log(1.0))), 0.2, 1.0),
        "decay_rate": jnp.clip(jnp.exp(jax.random.uniform(key_of[5], (QUDITS,), jnp.float32, math.log(0.2), math.log(2.0))), 0.2, 2.0),
        "dephasing": jnp.clip(jnp.exp(jax.random.uniform(key_of[6], (QUDITS,), jnp.float32, math.log(0.1), math.log(1.0))), 0.1, 1.0),
        "cross_kerr": jnp.clip(jnp.exp(jax.random.uniform(key_of[7], (PAIRS,), jnp.float32, math.log(0.05), math.log(0.3))), 0.05, 0.3),
    }


step_size = 0.01
highest = lax.Precision.HIGHEST

def ladder_tables(levels):
    lowering = np.eye(levels, k=1) * np.sqrt(np.arange(levels))[None, :]
    return (lowering, lowering + lowering.T)

def qudit_levels():
    return (LEVELS, LEVELS, LEVELS, LAST_LEVELS)

def on_rows(matrix, operator, position):
    levels_all = qudit_levels()
    before = math.prod(levels_all[:position])
    behind = math.prod(levels_all[position + 1:])
    shaped = matrix.reshape(matrix.shape[0], before, levels_all[position], behind, matrix.shape[-1])
    applied = jnp.einsum('ab,xpbqc->xpaqc', operator, shaped, precision=highest)
    return applied.reshape(matrix.shape)

def on_columns(matrix, operator, position):
    levels_all = qudit_levels()
    before = math.prod(levels_all[:position])
    behind = math.prod(levels_all[position + 1:])
    shaped = matrix.reshape(matrix.shape[0], matrix.shape[1], before, levels_all[position], behind)
    applied = jnp.einsum('xrpbq,ba->xrpaq', shaped, operator, precision=highest)
    return applied.reshape(matrix.shape)

def occupations(flat_index):
    levels_all = qudit_levels()
    stride = ORDER
    counts = []
    for position in range(4):
        stride = stride // levels_all[position]
        counts.append((flat_index // stride % levels_all[position]).astype(jnp.float32))
    return counts

def drift_energy(counts, detuning, anharmonicity, cross_kerr):
    energy = jnp.zeros_like(counts[0])
    for position in range(4):
        occupied = counts[position]
        energy = energy + detuning[position] * occupied - 0.5 * anharmonicity[position] * occupied * (occupied - 1.0)
    pair_index = 0
    for first_qudit in range(4):
        for second_qudit in range(first_qudit + 1, 4):
            energy = energy - cross_kerr[pair_index] * counts[first_qudit] * counts[second_qudit]
            pair_index = pair_index + 1
    return energy

def diagonal_terms(row_index, column_index, detuning, anharmonicity, decay_rate, dephasing, cross_kerr):
    row_counts = occupations(row_index)
    column_counts = occupations(column_index)
    phase = drift_energy(row_counts, detuning, anharmonicity, cross_kerr)[:, None] - drift_energy(column_counts, detuning, anharmonicity, cross_kerr)[None, :]
    damping = jnp.zeros(phase.shape, jnp.float32)
    for position in range(4):
        row_level = row_counts[position][:, None]
        across = column_counts[position][None, :]
        damping = damping - 0.5 * decay_rate[position] * (row_level + across) - 0.5 * dephasing[position] * (row_level - across) ** 2
    return (damping, phase)

def generator(matrix, amplitudes, lowering, coupling, decay_rate, damping, phase):
    commutator = jnp.zeros_like(matrix)
    sandwich = jnp.zeros_like(matrix)
    for position in range(4):
        commutator = commutator + amplitudes[position] * (on_rows(matrix, coupling[position], position) - on_columns(matrix, coupling[position], position))
        sandwich = sandwich + decay_rate[position] * on_rows(on_columns(matrix, lowering[position], position), lowering[position].T, position)
    real_part = damping * matrix[0] - phase * matrix[1] - commutator[1] + sandwich[0]
    imag_part = damping * matrix[1] + phase * matrix[0] + commutator[0] + sandwich[1]
    return jnp.stack([real_part, imag_part])

def reference(terminal_adjoint, midpoint_state, controls, detuning, anharmonicity, decay_rate, dephasing, cross_kerr):
    lowering = []
    coupling = []
    for levels in qudit_levels():
        low_table, pair_table = ladder_tables(levels)
        lowering.append(jnp.asarray(low_table, jnp.float32))
        coupling.append(jnp.asarray(pair_table, jnp.float32))
    flat_index = jnp.arange(ORDER, dtype=jnp.int32)
    damping, phase = diagonal_terms(flat_index, flat_index, detuning, anharmonicity, decay_rate, dephasing, cross_kerr)

    def segment_run(inputs):
        terminal, states, amplitudes_all = inputs
        current = terminal
        gradients = [None] * STEPS
        for step_index in reversed(range(STEPS)):
            amplitudes = amplitudes_all[step_index]
            midpoint = current
            for sweep_index in range(SWEEPS):
                midpoint = current + 0.5 * step_size * generator(midpoint, amplitudes, lowering, coupling, decay_rate, damping, phase)
            density = states[step_index]
            values = []
            for position in range(4):
                bracket = on_rows(density, coupling[position], position) - on_columns(density, coupling[position], position)
                values.append(jnp.sum(midpoint[0] * bracket[1] - midpoint[1] * bracket[0]) / ORDER)
            gradients[step_index] = jnp.stack(values)
            current = current + step_size * generator(midpoint, amplitudes, lowering, coupling, decay_rate, damping, phase)
        return (current, jnp.stack(gradients))
    start_adjoint, control_gradient = lax.map(segment_run, (terminal_adjoint, midpoint_state, controls))
    following = jnp.concatenate([start_adjoint[1:], jnp.zeros_like(start_adjoint[:1])], axis=0)
    return (start_adjoint, terminal_adjoint - following, control_gradient)
```

```python
import jax
import jax.numpy as jnp
import numpy as np
from jax import lax
from jax.experimental import pallas as pl
from jax.experimental.pallas import tpu as pltpu
from jax.sharding import PartitionSpec as P


ORDER = 2048
STEP = 0.01
UNITS = 32
ROWS = 16
LANES = 128
TILES = 4
WIDTH = TILES * LANES
F32 = jnp.float32

GROUPS = [
    [4 * y + z for y in (0, 1) for z in (0, 1, 3, 2)],
    [4 * y + z for y in (3, 2) for z in (2, 3, 1, 0)],
]
Y_OUTER = {0: 3, 3: 0, 1: 2, 2: 1}
Y_INNER = {0: 1, 1: 0, 2: 3, 3: 2}


def pairs_y(flip):
    return [(4 * y + z, 4 * flip[y] + z) for y in range(4) for z in range(4)]


def pairs_z(flip):
    return [(4 * y + z, 4 * y + flip[z]) for y in range(4) for z in range(4)]


PERM_I0 = pairs_y(Y_OUTER)
PERM_I2 = pairs_y(Y_INNER)
PERM_J0 = pairs_z(Y_OUTER)
PERM_J1 = pairs_z(Y_INNER)
PERM_CORNER = [(4 * y + z, 4 * Y_OUTER[y] + Y_OUTER[z]) for y in (0, 1) for z in (0, 1)]
ROOTS = np.sqrt(np.arange(16)).astype(np.float32)


class Place:
    def __init__(self):
        row = lax.axis_index("row")
        y = row // 4
        z = row % 4
        self.upper = y // 2
        self.gi2 = jnp.where((y == 1) | (y == 2), 1, 0)
        self.gj0 = z // 2
        self.gj1 = jnp.where((z == 1) | (z == 2), 1, 0)


def unit_at(p, i1):
    h = i1 // 4
    odd = p % 2
    return ((p // 2) * 4 + jnp.where(odd == 1, 3 - h, h)) * 4 + i1 % 4


def iotas():
    lane = lax.broadcasted_iota(jnp.int32, (ROWS, LANES), 1)
    sub = lax.broadcasted_iota(jnp.int32, (ROWS, LANES), 0)
    return lane, sub


class Tables:
    def __init__(self, place):
        lane, sub = iotas()
        low1 = lane // 32
        self.j1 = (low1 + 4 * place.gj1).astype(F32)
        self.j2 = ((lane // 4) % 8).astype(F32)
        self.j3 = (lane % 4).astype(F32)
        low2 = sub // 4
        self.i2 = (low2 + 4 * place.gi2).astype(F32)
        self.i3 = (sub % 4).astype(F32)
        self.c1p = jnp.where(low1 > 0, jnp.sqrt(self.j1), 0.0)
        self.c1m = jnp.where(low1 < 3, jnp.sqrt(self.j1 + 1.0), 0.0)
        self.c2p = jnp.sqrt(self.j2)
        self.c2m = jnp.where(self.j2 < 7.0, jnp.sqrt(self.j2 + 1.0), 0.0)
        self.c3p = jnp.sqrt(self.j3)
        self.c3m = jnp.where(self.j3 < 3.0, jnp.sqrt(self.j3 + 1.0), 0.0)
        self.r2p = jnp.where(low2 > 0, jnp.sqrt(self.i2), 0.0)
        self.r2m = jnp.where(low2 < 3, jnp.sqrt(self.i2 + 1.0), 0.0)
        self.r3p = jnp.sqrt(self.i3)
        self.r3m = jnp.where(self.i3 < 3.0, jnp.sqrt(self.i3 + 1.0), 0.0)
        edge1 = jnp.where(place.gj1 == 1, 0, 3)
        edge2 = jnp.where(place.gi2 == 1, 0, 3)
        self.edge1 = edge1
        self.at1 = (low1 == edge1).astype(F32)
        self.at2 = (low2 == edge2).astype(F32)


def drift(levels, detuning, anharmonicity, cross_kerr):
    total = 0.0
    for q in range(4):
        n = levels[q]
        total = total + detuning[q] * n - 0.5 * anharmonicity[q] * n * (n - 1.0)
    k = 0
    for a in range(4):
        for b in range(a + 1, 4):
            total = total - cross_kerr[k] * levels[a] * levels[b]
            k += 1
    return total


def decay_part(levels, decay, dephasing):
    total = 0.0
    for q in range(4):
        n = levels[q]
        total = total - 0.5 * decay[q] * n - 0.5 * dephasing[q] * n * n
    return total


def tile(ref, unit, c, t):
    return ref[unit, c, :, t * LANES : (t + 1) * LANES]


def level_of(place, p):
    return jnp.where(place.upper == 1, 7 - p, p)


def local_kernel(scale, with_gradient, *refs):
    if with_gradient:
        (z, base, rho, amp, det, anh, dec, dep, kerr, roots, out, sums) = refs
    else:
        (z, base, amp, det, anh, dec, dep, kerr, roots, out) = refs
    place = Place()
    tb = Tables(place)
    up = place.upper == 1
    detuning = [det[0, q] for q in range(4)]
    anharm = [anh[0, q] for q in range(4)]
    decay = [dec[0, q] for q in range(4)]
    dephasing = [dep[0, q] for q in range(4)]
    cross = [kerr[0, k] for k in range(6)]
    u = [amp[0, q] for q in range(4)]
    column_energy = []
    column_decay = []
    for t in range(TILES):
        j0 = (4 * place.gj0 + t).astype(F32)
        levels = [j0, tb.j1, tb.j2, tb.j3]
        column_energy.append(drift(levels, detuning, anharm, cross))
        column_decay.append(decay_part(levels, decay, dephasing))
    cross2 = dephasing[2] * tb.i2
    cross3 = dephasing[3] * tb.i3
    s2p = decay[2] * tb.r2p
    s3p = decay[3] * tb.r3p

    def step(n, carry):
        p = n // 8
        i1 = n % 8
        here = unit_at(p, i1)
        i0 = level_of(place, p)
        below = jnp.where(up, p + 1, p - 1)
        above = jnp.where(up, p - 1, p + 1)
        below_in = (below >= 0) & (below <= 3)
        above_in = (above >= 0) & (above <= 3)
        at_below = unit_at(jnp.clip(below, 0, 3), i1)
        at_above = unit_at(jnp.clip(above, 0, 3), i1)
        root_below = jnp.where(below_in, roots[0, i0], 0.0)
        root_above = jnp.where(above_in, roots[0, i0 + 1], 0.0)
        at_less = unit_at(p, jnp.maximum(i1 - 1, 0))
        at_more = unit_at(p, jnp.minimum(i1 + 1, 7))
        root_less = roots[0, i1]
        root_more = jnp.where(i1 < 7, roots[0, i1 + 1], 0.0)
        i0f = i0.astype(F32)
        i1f = i1.astype(F32)
        rows = [i0f, i1f, tb.i2, tb.i3]
        row_energy = drift(rows, detuning, anharm, cross)
        row_decay = decay_part(rows, decay, dephasing)
        new_carry = list(carry)
        for t in range(TILES):
            j0 = 4 * place.gj0 + t
            root_left = roots[0, j0]
            root_right = roots[0, j0 + 1]
            comm = []
            sand = []
            values = []
            parts = []
            for c in range(2):
                m = tile(z, here, c, t)
                values.append(m)
                w1 = tb.c1p * pltpu.roll(m, 32, 1)
                w2 = tb.c2p * pltpu.roll(m, 4, 1)
                w3 = tb.c3p * pltpu.roll(m, 1, 1)
                less = tile(z, at_less, c, t)
                k0 = root_below * tile(z, at_below, c, t) + root_above * tile(z, at_above, c, t)
                if t > 0:
                    k0 = k0 - root_left * tile(z, here, c, t - 1)
                if t < TILES - 1:
                    k0 = k0 - root_right * tile(z, here, c, t + 1)
                k1 = (
                    root_less * less
                    + root_more * tile(z, at_more, c, t)
                    - w1
                    - tb.c1m * pltpu.roll(m, LANES - 32, 1)
                )
                k2 = (
                    tb.r2p * pltpu.roll(m, 4, 0)
                    + tb.r2m * pltpu.roll(m, ROWS - 4, 0)
                    - w2
                    - tb.c2m * pltpu.roll(m, LANES - 4, 1)
                )
                k3 = (
                    tb.r3p * pltpu.roll(m, 1, 0)
                    + tb.r3m * pltpu.roll(m, ROWS - 1, 0)
                    - w3
                    - tb.c3m * pltpu.roll(m, LANES - 1, 1)
                )
                parts.append((k0, k1, k2, k3))
                comm.append(u[0] * k0 + u[1] * k1 + u[2] * k2 + u[3] * k3)
                s = (
                    (decay[1] * root_less) * (tb.c1p * pltpu.roll(less, 32, 1))
                    + s2p * pltpu.roll(w2, 4, 0)
                    + s3p * pltpu.roll(w3, 1, 0)
                )
                if t > 0:
                    s = s + (decay[0] * root_below * root_left) * tile(z, at_below, c, t - 1)
                sand.append(s)
            phase = row_energy - column_energy[t]
            damping = (
                row_decay
                + column_decay[t]
                + (dephasing[0] * i0f) * j0.astype(F32)
                + (dephasing[1] * i1f) * tb.j1
                + cross2 * tb.j2
                + cross3 * tb.j3
            )
            x, y = values
            lanes = slice(t * LANES, (t + 1) * LANES)
            out[here, 0, :, lanes] = tile(base, here, 0, t) + scale * (
                damping * x - phase * y - comm[1] + sand[0]
            )
            out[here, 1, :, lanes] = tile(base, here, 1, t) + scale * (
                damping * y + phase * x + comm[0] + sand[1]
            )
            if with_gradient:
                re = tile(rho, here, 0, t)
                im = tile(rho, here, 1, t)
                for q in range(4):
                    new_carry[q] = new_carry[q] + parts[0][q] * im - parts[1][q] * re
        return tuple(new_carry)

    start = tuple(jnp.zeros((ROWS, LANES), F32) for _ in range(4)) if with_gradient else ()
    total = lax.fori_loop(0, UNITS, step, start)
    if with_gradient:
        for q in range(4):
            sums[q] = total[q]


def put_slabs(place, tb, p, pair, both, s_i0, s_i2, s_j0, s_j1, s_c):
    lane, _ = iotas()
    half = lax.broadcasted_iota(jnp.int32, (8, LANES), 0) < 4
    block = lane // 32
    gj0 = place.gj0 == 1
    gi2 = place.gi2 == 1
    for par in range(2):
        i1 = 2 * pair + par
        n = p * 8 + i1
        for c in range(2):
            tiles = both[par][c]
            if p == 3:
                for t in range(TILES):
                    s_i0[i1, c, :, t * LANES : (t + 1) * LANES] = tiles[t]
                s_c[i1, c] = tiles[TILES - 1]
            s_j0[n, c] = jnp.where(gj0, tiles[0], tiles[TILES - 1])
            packed = jnp.zeros((ROWS, LANES), F32)
            for t in range(TILES):
                turned = jnp.where(
                    place.gj1 == 1,
                    pltpu.roll(tiles[t], (32 * t) % LANES, 1) if t else tiles[t],
                    pltpu.roll(tiles[t], (32 * (t + 1)) % LANES, 1) if t < 3 else tiles[t],
                )
                packed = jnp.where(block == t, turned, packed)
            s_j1[n, c] = packed
    for c in range(2):
        for t in range(TILES):
            even, odd = both[0][c][t], both[1][c][t]
            first = jnp.where(gi2, even[0:8], pltpu.roll(even[8:16], 4, 0))
            second = jnp.where(gi2, pltpu.roll(odd[0:8], 4, 0), odd[8:16])
            s_i2[p * 4 + pair, c, :, t * LANES : (t + 1) * LANES] = jnp.where(half, first, second)


def slab_kernel(z, s_i0, s_i2, s_j0, s_j1, s_c):
    place = Place()
    tb = Tables(place)
    for p in range(4):

        def step(pair, carry, p=p):
            both = [
                [[tile(z, unit_at(p, 2 * pair + par), c, t) for t in range(TILES)] for c in range(2)]
                for par in range(2)
            ]
            put_slabs(place, tb, p, pair, both, s_i0, s_i2, s_j0, s_j1, s_c)
            return carry

        lax.fori_loop(0, 4, step, 0)


def edge_kernel(scale, last, *refs):
    if last:
        (part, h_i0, h_i2, h_j0, h_j1, h_c, rho, sums, amp, dec, roots, out, grad) = refs
    else:
        (part, h_i0, h_i2, h_j0, h_j1, h_c, amp, dec, roots, out, *slabs) = refs
    place = Place()
    tb = Tables(place)
    up = place.upper == 1
    upf = place.upper.astype(F32)
    gi2 = place.gi2 == 1
    gj0f = place.gj0.astype(F32)
    gj1f = place.gj1.astype(F32)
    gi2f = place.gi2.astype(F32)
    decay = [dec[0, q] for q in range(4)]
    u = [amp[0, q] for q in range(4)]
    total = tuple(jnp.zeros((ROWS, LANES), F32) for _ in range(3))
    s1_base = (decay[1] * 2.0 * gj1f) * tb.at1
    s2_base = (decay[2] * 2.0 * gi2f) * tb.at2 * tb.c2p
    k1_mask = -2.0 * tb.at1
    k2_mask = 2.0 * tb.at2
    for p in range(4):

        def step(pair, carry, p=p):
            i0 = jnp.where(up, 7 - p, p)
            below = jnp.where(up, p + 1, p - 1)
            below_in = (below >= 0) & (below <= 3)
            below = jnp.clip(below, 0, 3)
            root_below = jnp.where(below_in, roots[0, i0], 0.0)
            both = []
            acc = list(carry)
            for par in range(2):
                i1 = 2 * pair + par
                here = unit_at(p, i1)
                n = p * 8 + i1
                root_less = roots[0, i1]
                n_less = p * 8 + jnp.maximum(i1 - 1, 0)
                new = [[], []]
                for t in range(TILES):
                    j0 = 4 * place.gj0 + t
                    lanes = slice(t * LANES, (t + 1) * LANES)
                    comm = []
                    sand = []
                    parts = []
                    for c in range(2):
                        small = h_i2[p * 4 + pair, c, :, lanes]
                        turned = pltpu.roll(small, 4, 0)
                        small = jnp.where(gi2, turned, small) if par else jnp.where(gi2, small, turned)
                        both2 = jnp.concatenate([small, small], axis=0)
                        k2 = k2_mask * both2
                        s = s2_base * pltpu.roll(both2, 4, 1)
                        k1 = k1_mask * pltpu.roll(h_j1[n, c], (32 * (tb.edge1 - t)) % LANES, 1)
                        s = s + (root_less * s1_base) * pltpu.roll(h_j1[n_less, c], (32 * (tb.edge1 - t)) % LANES, 1)
                        k0 = None
                        if p == 3:
                            k0 = 2.0 * h_i0[i1, c, :, lanes]
                            if t > 0:
                                s = s + (decay[0] * 2.0 * upf * roots[0, j0]) * h_i0[
                                    i1, c, :, (t - 1) * LANES : t * LANES
                                ]
                            else:
                                s = s + (decay[0] * 4.0 * upf * gj0f) * h_c[i1, c]
                        if t == 0 or t == TILES - 1:
                            on = gj0f if t == 0 else 1.0 - gj0f
                            term = (2.0 * on) * h_j0[n, c]
                            k0 = -term if k0 is None else k0 - term
                        if t == 0:
                            s = s + (decay[0] * 2.0 * gj0f * root_below) * h_j0[below * 8 + i1, c]
                        k = u[1] * k1 + u[2] * k2
                        if k0 is not None:
                            k = k + u[0] * k0
                        comm.append(k)
                        sand.append(s)
                        parts.append((k0, k1, k2))
                    x = tile(part, here, 0, t) + scale * (sand[0] - comm[1])
                    y = tile(part, here, 1, t) + scale * (sand[1] + comm[0])
                    out[here, 0, :, lanes] = x
                    out[here, 1, :, lanes] = y
                    new[0].append(x)
                    new[1].append(y)
                    if last:
                        re = tile(rho, here, 0, t)
                        im = tile(rho, here, 1, t)
                        for q in range(3):
                            if parts[0][q] is not None:
                                acc[q] = acc[q] + parts[0][q] * im - parts[1][q] * re
                both.append(new)
            if not last:
                put_slabs(place, tb, p, pair, both, *slabs)
            return tuple(acc)

        total = lax.fori_loop(0, 4, step, total)
    if last:
        for q in range(4):
            value = sums[q] + total[q] if q < 3 else sums[q]
            grad[q : q + 1] = jnp.sum(value, axis=0, keepdims=True)
        grad[4:8] = jnp.zeros((4, LANES), F32)


def pack_kernel(x, out):
    upper = lax.axis_index("row") // 8
    for gi2 in range(2):
        for g in range(4):
            k = 4 * gi2 + jnp.where(upper == 1, 3 - g, g)
            gj0, gj1 = g // 2, g % 2
            for c in range(2):
                for t in range(TILES):
                    start = gj0 * 1024 + t * 256 + gj1 * 128
                    out[k, 0, c, :, t * LANES : (t + 1) * LANES] = x[
                        c, gi2 * 16 : gi2 * 16 + 16, start : start + LANES
                    ]


def unpack_kernel(subtract, *refs):
    if subtract:
        x, base, out = refs
    else:
        x, out = refs
    upper = lax.axis_index("row") // 8
    for gi2 in range(2):
        for g in range(4):
            k = 4 * gi2 + jnp.where(upper == 1, 3 - g, g)
            gj0, gj1 = g // 2, g % 2
            for c in range(2):
                for t in range(TILES):
                    start = gj0 * 1024 + t * 256 + gj1 * 128
                    value = x[k, 0, c, :, t * LANES : (t + 1) * LANES]
                    rows = slice(gi2 * 16, gi2 * 16 + 16)
                    if subtract:
                        value = base[c, rows, start : start + LANES] - value
                    out[c, rows, start : start + LANES] = value


VMEM = pl.BlockSpec(memory_space=pltpu.VMEM)
SMEM = pl.BlockSpec(memory_space=pltpu.SMEM)
PARAMS = pltpu.CompilerParams(vmem_limit_bytes=48 * 1024 * 1024)
UNIT_SHAPE = (UNITS, 2, ROWS, WIDTH)
SLAB_SHAPES = [
    (8, 2, ROWS, WIDTH),
    (16, 2, 8, WIDTH),
    (UNITS, 2, ROWS, LANES),
    (UNITS, 2, ROWS, LANES),
    (8, 2, ROWS, LANES),
]


def shape(dims):
    return jax.ShapeDtypeStruct(dims, F32)


def cost(flops, bytes_accessed):
    return pl.CostEstimate(flops=flops, bytes_accessed=bytes_accessed, transcendentals=0)


PACKED_BLOCK = pl.BlockSpec((8, 1, 2, ROWS, WIDTH), lambda a: (0, a, 0, 0, 0))
PLAIN_BLOCK = pl.BlockSpec((2, 32, ORDER), lambda a: (0, a, 0))
PACKED_SHAPE = (8, 4, 2, ROWS, WIDTH)


def pack(x):
    return pl.pallas_call(
        pack_kernel,
        out_shape=shape(PACKED_SHAPE),
        grid=(4,),
        in_specs=[PLAIN_BLOCK],
        out_specs=PACKED_BLOCK,
        compiler_params=PARAMS,
        cost_estimate=cost(0, 4 << 20),
        name="pack_blocks",
    )(x)


def unpack(x, base=None):
    subtract = base is not None
    args = (x, base) if subtract else (x,)

    def kernel(*refs):
        unpack_kernel(subtract, *refs)

    return pl.pallas_call(
        kernel,
        out_shape=shape((2, 128, ORDER)),
        grid=(4,),
        in_specs=[PACKED_BLOCK] + ([PLAIN_BLOCK] if subtract else []),
        out_specs=PLAIN_BLOCK,
        compiler_params=PARAMS,
        cost_estimate=cost(0, 4 << 20),
        name="unpack_blocks",
    )(*args)


def regroup(x):
    return lax.all_to_all(x, "row", 0, 0, axis_index_groups=GROUPS, tiled=True)


def exchange(slabs):
    s_i0, s_i2, s_j0, s_j1, s_c = slabs
    return (
        lax.ppermute(s_i0, "row", PERM_I0),
        lax.ppermute(s_i2, "row", PERM_I2),
        lax.ppermute(s_j0, "row", PERM_J0),
        lax.ppermute(s_j1, "row", PERM_J1),
        lax.ppermute(s_c, "row", PERM_CORNER),
    )


def slabs_of(z):
    return pl.pallas_call(
        slab_kernel,
        out_shape=[shape(s) for s in SLAB_SHAPES],
        in_specs=[VMEM],
        out_specs=[VMEM] * 5,
        compiler_params=PARAMS,
        cost_estimate=cost(0, 4 << 20),
        name="slabs",
    )(z)


def local_terms(scale, z, base, scalars, rho=None):
    grad = rho is not None
    args = [z, base] + ([rho] if grad else []) + list(scalars)
    outs = [shape(UNIT_SHAPE)] + ([shape((4, ROWS, LANES))] if grad else [])

    def kernel(*refs):
        local_kernel(scale, grad, *refs)

    return pl.pallas_call(
        kernel,
        out_shape=outs,
        in_specs=[VMEM] * (3 if grad else 2) + [SMEM] * len(scalars),
        out_specs=[VMEM] * len(outs),
        compiler_params=PARAMS,
        cost_estimate=cost(60 * 512 * 1024, 6 << 20),
        name="local_terms",
    )(*args)


def edge_terms(scale, part, halos, scalars, rho=None, sums=None):
    last = rho is not None
    args = [part, *halos] + ([rho, sums] if last else []) + list(scalars)
    outs = [shape(UNIT_SHAPE)]
    if last:
        outs += [shape((8, LANES))]
    else:
        outs += [shape(s) for s in SLAB_SHAPES]

    def kernel(*refs):
        edge_kernel(scale, last, *refs)

    return pl.pallas_call(
        kernel,
        out_shape=outs,
        in_specs=[VMEM] * (len(args) - len(scalars)) + [SMEM] * len(scalars),
        out_specs=[VMEM] * len(outs),
        compiler_params=PARAMS,
        cost_estimate=cost(10 * 512 * 1024, 6 << 20),
        name="edge_terms",
    )(*args)


def body(
    terminal_adjoint,
    midpoint_state,
    controls,
    detuning,
    anharmonicity,
    decay_rate,
    dephasing,
    cross_kerr,
):
    amp = controls[0]
    dec = decay_rate[None]
    roots = jnp.asarray(ROOTS)[None]
    full = (amp, detuning[None], anharmonicity[None], dec, dephasing[None], cross_kerr[None], roots)
    few = (amp, dec, roots)
    terminal = terminal_adjoint[0]
    base = regroup(pack(terminal)).reshape(UNIT_SHAPE)
    slabs = slabs_of(base)
    rho = regroup(pack(midpoint_state[0, 0])).reshape(UNIT_SHAPE)
    current = base
    for sweep in range(2):
        halos = exchange(slabs)
        (part,) = local_terms(0.5 * STEP, current, base, full)
        current, *slabs = edge_terms(0.5 * STEP, part, halos, few)
    halos = exchange(slabs)
    part, sums = local_terms(STEP, current, base, full, rho)
    final, grad = edge_terms(STEP, part, halos, few, rho, sums)
    back = regroup(final.reshape(PACKED_SHAPE))
    for perm in (PERM_I0, PERM_I2, PERM_J0, PERM_J1):
        grad = grad + lax.ppermute(grad, "row", perm)
    following = lax.ppermute(back, "seg", [(i + 1, i) for i in range(7)])
    start = unpack(back)
    defect = unpack(following, terminal)
    totals = jnp.sum(grad[:4], axis=1) / ORDER
    return start[None], defect[None], totals[None, None]


def solution(mesh):
    return jax.shard_map(
        body,
        mesh=mesh,
        in_specs=(
            P("seg", None, "row", None),
            P("seg", None, None, "row", None),
            P("seg", None, None),
            P(),
            P(),
            P(),
            P(),
            P(),
        ),
        out_specs=(P("seg", None, "row", None), P("seg", None, "row", None), P("seg", None, None)),
        check_vma=False,
    )
```

```python
import jax
import jax.numpy as jnp
import numpy as np
from jax import lax
from jax.experimental import pallas as pl
from jax.experimental.pallas import tpu as pltpu
from jax.sharding import PartitionSpec as P


ORDER = 2048
STEP = 0.01
UNITS = 32
ROWS = 16
LANES = 128
TILES = 4
WIDTH = TILES * LANES
F32 = jnp.float32

GROUPS = [
    [4 * y + z for y in (0, 1) for z in (0, 1, 3, 2)],
    [4 * y + z for y in (3, 2) for z in (2, 3, 1, 0)],
]
Y_OUTER = {0: 3, 3: 0, 1: 2, 2: 1}
Y_INNER = {0: 1, 1: 0, 2: 3, 3: 2}


def pairs_y(flip):
    return [(4 * y + z, 4 * flip[y] + z) for y in range(4) for z in range(4)]


def pairs_z(flip):
    return [(4 * y + z, 4 * y + flip[z]) for y in range(4) for z in range(4)]


PERM_I0 = pairs_y(Y_OUTER)
PERM_I2 = pairs_y(Y_INNER)
PERM_J0 = pairs_z(Y_OUTER)
PERM_J1 = pairs_z(Y_INNER)
PERM_CORNER = [(4 * y + z, 4 * Y_OUTER[y] + Y_OUTER[z]) for y in (0, 1) for z in (0, 1)]
ROOTS = np.sqrt(np.arange(16)).astype(np.float32)


class Place:
    def __init__(self):
        row = lax.axis_index("row")
        y = row // 4
        z = row % 4
        self.upper = y // 2
        self.gi2 = jnp.where((y == 1) | (y == 2), 1, 0)
        self.gj0 = z // 2
        self.gj1 = jnp.where((z == 1) | (z == 2), 1, 0)
        gray = z ^ (z // 2)
        self.slot = jnp.where(self.upper == 1, 4 * (3 - y) + 3 - gray, 4 * y + gray)


def unit_at(p, i1):
    h = i1 // 4
    odd = p % 2
    return ((p // 2) * 4 + jnp.where(odd == 1, 3 - h, h)) * 4 + i1 % 4


def iotas():
    lane = lax.broadcasted_iota(jnp.int32, (ROWS, LANES), 1)
    sub = lax.broadcasted_iota(jnp.int32, (ROWS, LANES), 0)
    return lane, sub


class Tables:
    def __init__(self, place):
        lane, sub = iotas()
        low1 = lane // 32
        self.j1 = (low1 + 4 * place.gj1).astype(F32)
        self.j2 = ((lane // 4) % 8).astype(F32)
        self.j3 = (lane % 4).astype(F32)
        low2 = sub // 4
        self.i2 = (low2 + 4 * place.gi2).astype(F32)
        self.i3 = (sub % 4).astype(F32)
        self.c1p = jnp.where(low1 > 0, jnp.sqrt(self.j1), 0.0)
        self.c1m = jnp.where(low1 < 3, jnp.sqrt(self.j1 + 1.0), 0.0)
        self.c2p = jnp.sqrt(self.j2)
        self.c2m = jnp.where(self.j2 < 7.0, jnp.sqrt(self.j2 + 1.0), 0.0)
        self.c3p = jnp.sqrt(self.j3)
        self.c3m = jnp.where(self.j3 < 3.0, jnp.sqrt(self.j3 + 1.0), 0.0)
        self.r2p = jnp.where(low2 > 0, jnp.sqrt(self.i2), 0.0)
        self.r2m = jnp.where(low2 < 3, jnp.sqrt(self.i2 + 1.0), 0.0)
        self.r3p = jnp.sqrt(self.i3)
        self.r3m = jnp.where(self.i3 < 3.0, jnp.sqrt(self.i3 + 1.0), 0.0)
        edge1 = jnp.where(place.gj1 == 1, 0, 3)
        edge2 = jnp.where(place.gi2 == 1, 0, 3)
        self.edge1 = edge1
        self.at1 = (low1 == edge1).astype(F32)
        self.at2 = (low2 == edge2).astype(F32)


def drift(levels, detuning, anharmonicity, cross_kerr):
    total = 0.0
    for q in range(4):
        n = levels[q]
        total = total + detuning[q] * n - 0.5 * anharmonicity[q] * n * (n - 1.0)
    k = 0
    for a in range(4):
        for b in range(a + 1, 4):
            total = total - cross_kerr[k] * levels[a] * levels[b]
            k += 1
    return total


def decay_part(levels, decay, dephasing):
    total = 0.0
    for q in range(4):
        n = levels[q]
        total = total - 0.5 * decay[q] * n - 0.5 * dephasing[q] * n * n
    return total


def tile(ref, unit, c, t):
    return ref[unit, c, :, t * LANES : (t + 1) * LANES]


def level_of(place, p):
    return jnp.where(place.upper == 1, 7 - p, p)


def unit_neighbours(place, roots, p, i1):
    up = place.upper == 1
    i0 = level_of(place, p)
    below = jnp.where(up, p + 1, p - 1)
    above = jnp.where(up, p - 1, p + 1)
    root_below = jnp.where((below >= 0) & (below <= 3), roots[0, i0], 0.0)
    root_above = jnp.where((above >= 0) & (above <= 3), roots[0, i0 + 1], 0.0)
    return (
        i0,
        (unit_at(jnp.clip(below, 0, 3), i1), root_below),
        (unit_at(jnp.clip(above, 0, 3), i1), root_above),
        (unit_at(p, jnp.maximum(i1 - 1, 0)), roots[0, i1]),
        (unit_at(p, jnp.minimum(i1 + 1, 7)), jnp.where(i1 < 7, roots[0, i1 + 1], 0.0)),
    )


def local_kernel(scale, n, *refs):
    z, base = refs[:2]
    if n:
        state, *received = refs[2:6]
        *scalars, out, next_state = refs[6:15] if n == 1 else (*refs[6:14], refs[16])
        copy_state(n - 1, state, received, next_state, lambda r: r)
    else:
        *scalars, out = refs[2:]
    writes = []
    if n == 2:
        z_out, state_out = refs[14:16]
        sems = refs[17]
        writes = [
            pltpu.make_async_copy(z, z_out, sems.at[0]),
            pltpu.make_async_copy(next_state, state_out, sems.at[1]),
        ]
    start_all(writes)
    amp, det, anh, dec, dep, kerr, roots = scalars
    place = Place()
    tb = Tables(place)
    detuning = [det[0, q] for q in range(4)]
    anharm = [anh[0, q] for q in range(4)]
    decay = [dec[0, q] for q in range(4)]
    dephasing = [dep[0, q] for q in range(4)]
    cross = [kerr[0, k] for k in range(6)]
    u = [amp[0, q] for q in range(4)]
    column_energy = []
    column_decay = []
    for t in range(TILES):
        j0 = (4 * place.gj0 + t).astype(F32)
        levels = [j0, tb.j1, tb.j2, tb.j3]
        column_energy.append(drift(levels, detuning, anharm, cross))
        column_decay.append(decay_part(levels, decay, dephasing))
    cross2 = dephasing[2] * tb.i2
    cross3 = dephasing[3] * tb.i3
    c1m, c2m, c3m = u[1] * tb.c1m, u[2] * tb.c2m, u[3] * tb.c3m
    c1p, c2p, c3p = u[1] * tb.c1p, u[2] * tb.c2p, u[3] * tb.c3p
    r2m, r3m = u[2] * tb.r2m, u[3] * tb.r3m
    r2p, r3p = u[2] * tb.r2p, u[3] * tb.r3p
    d2p, d3p = decay[2] * tb.r2p, decay[3] * tb.r3p

    def step(n, carry):
        p = n // 8
        i1 = n % 8
        here = unit_at(p, i1)
        i0, below, above, less, more = unit_neighbours(place, roots, p, i1)
        i0f = i0.astype(F32)
        i1f = i1.astype(F32)
        rows = [i0f, i1f, tb.i2, tb.i3]
        row_energy = drift(rows, detuning, anharm, cross)
        row_decay = decay_part(rows, decay, dephasing)
        d1p = (decay[1] * less[1]) * tb.c1p
        for t in range(TILES):
            j0 = 4 * place.gj0 + t
            root_left = roots[0, j0]
            root_right = roots[0, j0 + 1]
            comm = []
            sand = []
            values = []
            for c in range(2):
                m = tile(z, here, c, t)
                values.append(m)
                turned2 = pltpu.roll(m, 4, 1)
                turned3 = pltpu.roll(m, 1, 1)
                row1 = tile(z, less[0], c, t)
                row0 = tile(z, below[0], c, t)
                k = (u[0] * below[1]) * row0 + (u[0] * above[1]) * tile(z, above[0], c, t)
                k = k + (u[1] * less[1]) * row1 + (u[1] * more[1]) * tile(z, more[0], c, t)
                if t > 0:
                    k = k - (u[0] * root_left) * tile(z, here, c, t - 1)
                if t < TILES - 1:
                    k = k - (u[0] * root_right) * tile(z, here, c, t + 1)
                k = k + r2p * pltpu.roll(m, 4, 0) + r2m * pltpu.roll(m, ROWS - 4, 0)
                k = k + r3p * pltpu.roll(m, 1, 0) + r3m * pltpu.roll(m, ROWS - 1, 0)
                k = k - c1p * pltpu.roll(m, 32, 1) - c1m * pltpu.roll(m, LANES - 32, 1)
                k = k - c2p * turned2 - c2m * pltpu.roll(m, LANES - 4, 1)
                k = k - c3p * turned3 - c3m * pltpu.roll(m, LANES - 1, 1)
                comm.append(k)
                s = (
                    d1p * pltpu.roll(row1, 32, 1)
                    + d2p * pltpu.roll(tb.c2p * turned2, 4, 0)
                    + d3p * pltpu.roll(tb.c3p * turned3, 1, 0)
                )
                if t > 0:
                    s = s + (decay[0] * below[1] * root_left) * tile(z, below[0], c, t - 1)
                sand.append(s)
            phase = row_energy - column_energy[t]
            damping = (
                row_decay
                + (column_decay[t] + (dephasing[0] * i0f) * j0.astype(F32))
                + (dephasing[1] * i1f) * tb.j1
                + cross2 * tb.j2
                + cross3 * tb.j3
            )
            x, y = values
            lanes = slice(t * LANES, (t + 1) * LANES)
            out[here, 0, :, lanes] = tile(base, here, 0, t) + scale * (
                damping * x - phase * y - comm[1] + sand[0]
            )
            out[here, 1, :, lanes] = tile(base, here, 1, t) + scale * (
                damping * y + phase * x + comm[0] + sand[1]
            )
        return carry

    lax.fori_loop(0, UNITS, step, 0)
    wait_all(writes)


PARTS = ((0, 1, 2), (3, 4, 5), (6, 7))
ROUTES = ((0, 1, 2), (2, 0, 1), (1, 2, 0))
EDGE = 64


def sent_slots(bit):
    return [r for r in range(8) if r >> bit & 1]


def merged_state(n, part, r):
    bit = ROUTES[n].index(part) if n >= 0 else 0
    if n < 0 or not r >> bit & 1:
        return None
    return bit, EDGE + sent_slots(bit).index(r) * len(PARTS[part]) * TILES


def state_entry(part, r):
    return (r * 8 + PARTS[part][0]) * TILES


def copy_state(n, state, received, out, slots):
    for r in range(8):
        for part in range(3):
            size = len(PARTS[part]) * TILES
            found = merged_state(n, part, r)
            source, first = (state, state_entry(part, r)) if found is None else (received[found[0]], found[1])
            out[pl.ds(state_entry(part, slots(r)), size)] = source[first : first + size]


def load_riders(n, state, received, carriers):
    for bit in range(3):
        part = ROUTES[n][bit]
        size = len(PARTS[part]) * TILES
        for at, r in enumerate(sent_slots(bit)):
            found = merged_state(n - 1, part, r)
            source, first = (state, state_entry(part, r)) if found is None else (received[found[0]], found[1])
            start = EDGE + at * size
            carriers[bit][start : start + size] = source[first : first + size]


def start_all(copies):
    for copy in copies:
        copy.start()


def wait_all(copies):
    for copy in copies:
        copy.wait()


def put_slabs(place, tb, p, pair, both, s_i0, s_j1, s_j0, s_i2, s_c):
    lane, _ = iotas()
    half = lax.broadcasted_iota(jnp.int32, (8, LANES), 0) < 4
    block = lane // 32
    gj0 = place.gj0 == 1
    gi2 = place.gi2 == 1
    for par in range(2):
        i1 = 2 * pair + par
        n = p * 8 + i1
        for c in range(2):
            tiles = both[par][c]
            if p == 3:
                for t in range(TILES):
                    s_i0[i1, c, :, t * LANES : (t + 1) * LANES] = tiles[t]
                s_c[i1, c] = tiles[TILES - 1]
            s_j0[2 * n + c] = jnp.where(gj0, tiles[0], tiles[TILES - 1])
            packed = None
            for t in range(TILES):
                turned = pltpu.roll(tiles[t], (32 * (t - tb.edge1)) % LANES, 1)
                packed = turned if packed is None else jnp.where(block == t, turned, packed)
            s_j1[2 * n + c] = packed
    for c in range(2):
        for t in range(TILES):
            even, odd = both[0][c][t], both[1][c][t]
            first = jnp.where(gi2, even[0:8], pltpu.roll(even[8:16], 4, 0))
            second = jnp.where(gi2, pltpu.roll(odd[0:8], 4, 0), odd[8:16])
            entry = ((p * 4 + pair) * 2 + c) * 2 + t // 2
            s_i2[entry, (t % 2) * 8 : (t % 2) * 8 + 8] = jnp.where(half, first, second)


def slab_kernel(z, state, s_i0, s_j1, s_j0, s_i2, s_c):
    place = Place()
    tb = Tables(place)
    load_riders(0, state, None, (s_j1, s_j0, s_i2))
    for p in range(4):

        def step(pair, carry, p=p):
            both = [
                [[tile(z, unit_at(p, 2 * pair + par), c, t) for t in range(TILES)] for c in range(2)]
                for par in range(2)
            ]
            put_slabs(place, tb, p, pair, both, s_i0, s_j1, s_j0, s_i2, s_c)
            return carry

        lax.fori_loop(0, 4, step, 0)


def i2_halo(place, h_i2, p, pair, par, c, t):
    small = h_i2[((p * 4 + pair) * 2 + c) * 2 + t // 2, (t % 2) * 8 : (t % 2) * 8 + 8]
    small = pltpu.roll(small, 4 * ((par + 1 + place.gi2) % 2), 0)
    return jnp.concatenate([small, small], axis=0)


def edge_kernel(scale, sent, *refs):
    last = sent is None
    part, h_i0, h_j1, h_j0, h_i2, h_c = refs[:6]
    if last:
        amp, dec, roots, out_all, out_rest, block, sems = refs[6:]
    else:
        state, amp, dec, roots, out, *slabs = refs[6:]
        load_riders(sent, state, (h_j1, h_j0, h_i2), slabs[1:4])
    place = Place()
    tb = Tables(place)
    up = place.upper == 1
    upf = place.upper.astype(F32)
    gj0f = place.gj0.astype(F32)
    gj1f = place.gj1.astype(F32)
    gi2f = place.gi2.astype(F32)
    copies = []
    decay = [scale * dec[0, q] for q in range(4)]
    u = [scale * amp[0, q] for q in range(4)]
    s1_base = (decay[1] * 2.0 * gj1f) * tb.at1
    s2_base = (decay[2] * 2.0 * gi2f) * tb.at2 * tb.c2p
    k1_mask = (-2.0 * u[1]) * tb.at1
    k2_mask = (2.0 * u[2]) * tb.at2

    def one(p, pair, par):
        i0 = jnp.where(up, 7 - p, p)
        below = jnp.where(up, p + 1, p - 1)
        below_in = (below >= 0) & (below <= 3)
        below = jnp.clip(below, 0, 3)
        root_below = jnp.where(below_in, roots[0, i0], 0.0)
        i1 = 2 * pair + par
        here = unit_at(p, i1)
        n = p * 8 + i1
        s1_less = roots[0, i1] * s1_base
        n_less = p * 8 + jnp.maximum(i1 - 1, 0)
        new = [[], []]
        for t in range(TILES):
            j0 = 4 * place.gj0 + t
            lanes = slice(t * LANES, (t + 1) * LANES)
            turn = (32 * (tb.edge1 - t)) % LANES
            comm = []
            sand = []
            for c in range(2):
                across = i2_halo(place, h_i2, p, pair, par, c, t)
                k = k2_mask * across + k1_mask * pltpu.roll(h_j1[2 * n + c], turn, 1)
                s = s2_base * pltpu.roll(across, 4, 1) + s1_less * pltpu.roll(h_j1[2 * n_less + c], turn, 1)
                if p == 3:
                    k = k + (2.0 * u[0]) * h_i0[i1, c, :, lanes]
                    if t > 0:
                        s = s + (decay[0] * 2.0 * upf * roots[0, j0]) * h_i0[
                            i1, c, :, (t - 1) * LANES : t * LANES
                        ]
                    else:
                        s = s + (decay[0] * 4.0 * upf * gj0f) * h_c[i1, c]
                if t == 0 or t == TILES - 1:
                    on = gj0f if t == 0 else 1.0 - gj0f
                    k = k - (2.0 * u[0] * on) * h_j0[2 * n + c]
                if t == 0:
                    s = s + (decay[0] * 2.0 * gj0f * root_below) * h_j0[2 * (below * 8 + i1) + c]
                comm.append(k)
                sand.append(s)
            new[0].append(tile(part, here, 0, t) + (sand[0] - comm[1]))
            new[1].append(tile(part, here, 1, t) + (sand[1] + comm[0]))
        return here, new

    for p in range(4):

        def step(pair, carry, p=p):
            both = []
            for par in range(2):
                here, new = one(p, pair, par)
                for c in range(2):
                    for t in range(TILES):
                        out[here, c, :, t * LANES : (t + 1) * LANES] = new[c][t]
                both.append(new)
            put_slabs(place, tb, p, pair, both, *slabs)
            return carry

        def last_step(h, carry, p=p):
            for a in range(4):
                here, new = one(p, 2 * h + a // 2, a % 2)
                for c in range(2):
                    for t in range(TILES):
                        lanes = slice(t * LANES, (t + 1) * LANES)
                        at = (2 * a + c) * ROWS
                        block[here // 4, at : at + ROWS, lanes] = new[c][t]
                        if 2 * a + c >= MOST:
                            at -= MOST * ROWS
                            out_rest[here // 4, at : at + ROWS, lanes] = new[c][t]
            return carry

        if last:
            lax.fori_loop(0, 2, last_step, 0)
            slots = pl.ds(2 * p, 2)
            copies.append(pltpu.make_async_copy(block.at[slots], out_all.at[slots], sems.at[p]))
            copies[-1].start()
        else:
            lax.fori_loop(0, 4, step, 0)
    wait_all(copies)


def gradient_kernel(z_in, h_i0, state_in, h_j1, h_j0, h_i2, roots, grad, z, state, rho, sems):
    reads = [pltpu.make_async_copy(state_in, state, sems.at[0]), pltpu.make_async_copy(z_in, z, sems.at[1])]
    start_all(reads)
    place = Place()
    tb = Tables(place)
    gj0f = place.gj0.astype(F32)
    wait_all(reads)
    copy_state(2, state, (h_j1, h_j0, h_i2), rho, lambda r: r ^ place.slot)
    k1_mask = -2.0 * tb.at1
    k2_mask = 2.0 * tb.at2

    def half_step(n, par, acc):
        p = n // 4
        pair = n % 4
        i1 = 2 * pair + par
        unit = p * 8 + i1
        here = unit_at(p, i1)
        _, below, above, less, more = unit_neighbours(place, roots, p, i1)
        outer = jnp.where(p == 3, 2.0, 0.0)
        for t in range(TILES):
            j0 = 4 * place.gj0 + t
            turn = (32 * (tb.edge1 - t)) % LANES
            for c in range(2):
                m = tile(z, here, c, t)
                k0 = below[1] * tile(z, below[0], c, t) + above[1] * tile(z, above[0], c, t)
                k0 = k0 + outer * h_i0[i1, c, :, t * LANES : (t + 1) * LANES]
                if t > 0:
                    k0 = k0 - roots[0, j0] * tile(z, here, c, t - 1)
                if t < TILES - 1:
                    k0 = k0 - roots[0, j0 + 1] * tile(z, here, c, t + 1)
                if t == 0 or t == TILES - 1:
                    on = gj0f if t == 0 else 1.0 - gj0f
                    k0 = k0 - (2.0 * on) * h_j0[2 * unit + c]
                k1 = less[1] * tile(z, less[0], c, t) + more[1] * tile(z, more[0], c, t)
                k1 = k1 - tb.c1p * pltpu.roll(m, 32, 1) - tb.c1m * pltpu.roll(m, LANES - 32, 1)
                k1 = k1 + k1_mask * pltpu.roll(h_j1[2 * unit + c], turn, 1)
                k2 = tb.r2p * pltpu.roll(m, 4, 0) + tb.r2m * pltpu.roll(m, ROWS - 4, 0)
                k2 = k2 - tb.c2p * pltpu.roll(m, 4, 1) - tb.c2m * pltpu.roll(m, LANES - 4, 1)
                k2 = k2 + k2_mask * i2_halo(place, h_i2, p, pair, par, c, t)
                k3 = tb.r3p * pltpu.roll(m, 1, 0) + tb.r3m * pltpu.roll(m, ROWS - 1, 0)
                k3 = k3 - tb.c3p * pltpu.roll(m, 1, 1) - tb.c3m * pltpu.roll(m, LANES - 1, 1)
                other = rho[(2 * here + 1 - c) * TILES + t]
                if c == 1:
                    other = -other
                acc = [acc[q] + k * other for q, k in enumerate((k0, k1, k2, k3))]
        return acc

    def step(n, carry):
        acc = list(carry)
        for par in range(2):
            acc = half_step(n, par, acc)
        return tuple(acc)

    total = lax.fori_loop(0, UNITS // 2, step, tuple(jnp.zeros((ROWS, LANES), F32) for _ in range(4)))
    for q in range(4):
        grad[:, q * LANES : (q + 1) * LANES] = total[q][0:8] + total[q][8:16]


def chunk_lanes(g, t):
    start = (g // 2) * 1024 + t * 256 + (g % 2) * 128
    return slice(start, start + LANES)


def slice_rows(a):
    return pl.ds(32 * a, 32)


def pack_kernel(x, out, plain, block, sems):
    upper = lax.axis_index("row") // 8
    reads = [
        pltpu.make_async_copy(x.at[:, slice_rows(a)], plain.at[:, slice_rows(a)], sems.at[a]) for a in range(4)
    ]
    writes = [pltpu.make_async_copy(block.at[:, a], out.at[:, a], sems.at[4 + a]) for a in range(4)]
    start_all(reads)
    for a in range(4):
        reads[a].wait()
        for gi2 in range(2):
            for g in range(4):
                k = 4 * gi2 + jnp.where(upper == 1, 3 - g, g)
                for c in range(2):
                    for t in range(TILES):
                        block[k, a, c, :, t * LANES : (t + 1) * LANES] = plain[
                            c, 32 * a + 16 * gi2 : 32 * a + 16 * gi2 + 16, chunk_lanes(g, t)
                        ]
        writes[a].start()
    wait_all(writes)


def deal_kernel(x, state):
    place = Place()
    for gi2 in range(2):
        for g in range(4):
            k = 4 * gi2 + jnp.where(place.upper == 1, 3 - g, g)
            r = k ^ place.slot
            for a in range(4):
                rows = slice(a * 32 + gi2 * 16, a * 32 + gi2 * 16 + 16)
                for c in range(2):
                    for t in range(TILES):
                        state[(r * 8 + a * 2 + c) * TILES + t] = x[c, rows, chunk_lanes(g, t)]


def join_kernel(blocks, grad, out, sems):
    rows = 16 * (8 - MOST)
    copies = [pltpu.make_async_copy(blocks, out.at[:, pl.ds(0, rows)], sems.at[8])]
    for k in range(8):
        copies.append(pltpu.make_async_copy(grad, out.at[k, pl.ds(rows, 8)], sems.at[k]))
    start_all(copies)
    wait_all(copies)


def undeal(upper, index, source, first, out, base=None):
    a, c = index // 2, index % 2
    for gi2 in range(2):
        rows = slice(32 * a + 16 * gi2, 32 * a + 16 * gi2 + 16)
        for g in range(4):
            k = 4 * gi2 + jnp.where(upper == 1, 3 - g, g)
            for t in range(TILES):
                lanes = chunk_lanes(g, t)
                value = source[k, first : first + 16, t * LANES : (t + 1) * LANES]
                if base is not None:
                    value = base[c, rows, lanes] - value
                out[c, rows, lanes] = value


def start_kernel(blocks, start, held, plain, sems):
    upper = lax.axis_index("row") // 8
    reads = [
        pltpu.make_async_copy(blocks.at[:, pl.ds(32 * a, 32)], held.at[:, pl.ds(32 * a, 32)], sems.at[a])
        for a in range(4)
    ]
    writes = [
        pltpu.make_async_copy(plain.at[:, slice_rows(a)], start.at[:, slice_rows(a)], sems.at[4 + a])
        for a in range(4)
    ]
    start_all(reads)
    for a in range(4):
        reads[a].wait()
        for c in range(2):
            undeal(upper, 2 * a + c, held, 32 * a + 16 * c, plain)
        writes[a].start()
    wait_all(writes)


def finish_kernel(most, rest, base, defect, held_most, held_rest, held_base, plain, sems):
    upper = lax.axis_index("row") // 8
    rows = 16 * (8 - MOST)
    reads = [
        pltpu.make_async_copy(rest.at[:, pl.ds(0, rows)], held_rest, sems.at[0]),
        pltpu.make_async_copy(most, held_most, sems.at[1]),
    ]
    order = (3, 2, 1, 0)
    for a in order:
        reads.append(
            pltpu.make_async_copy(base.at[:, slice_rows(a)], held_base.at[:, slice_rows(a)], sems.at[2 + a])
        )
    writes = [
        pltpu.make_async_copy(plain.at[:, slice_rows(a)], defect.at[:, slice_rows(a)], sems.at[6 + a])
        for a in order
    ]
    start_all(reads)
    reads[0].wait()
    for at, a in enumerate(order):
        if at == 1:
            reads[1].wait()
        reads[2 + at].wait()
        for c in range(2):
            index = 2 * a + c
            if index < MOST:
                undeal(upper, index, held_most, 16 * index, plain, held_base)
            else:
                undeal(upper, index, held_rest, 16 * (index - MOST), plain, held_base)
        writes[at].start()
    wait_all(writes)


VMEM = pl.BlockSpec(memory_space=pltpu.VMEM)
SMEM = pl.BlockSpec(memory_space=pltpu.SMEM)
ANY = pl.BlockSpec(memory_space=pl.ANY)
PARAMS = pltpu.CompilerParams(vmem_limit_bytes=16 * 1024 * 1024)
MOST = 5
UNIT_SHAPE = (UNITS, 2, ROWS, WIDTH)
PACKED_SHAPE = (8, 4, 2, ROWS, WIDTH)
STATE_SHAPE = (64 * TILES, ROWS, LANES)
PLAIN_SHAPE = (2, 128, ORDER)
BLOCKS_SHAPE = (8, 128, WIDTH)
MOST_SHAPE = (8, 16 * MOST, WIDTH)
REST_SHAPE = (8, 16 * (8 - MOST), WIDTH)
JOINED_SHAPE = (8, 16 * (8 - MOST) + 8, WIDTH)


def slab_shapes(n):
    riders = [4 * len(PARTS[ROUTES[n][bit]]) * TILES for bit in range(3)]
    return (
        [(8, 2, ROWS, WIDTH)]
        + [(EDGE + extra, ROWS, LANES) for extra in riders]
        + [(8, 2, ROWS, LANES)]
    )


def shape(dims):
    return jax.ShapeDtypeStruct(dims, F32)


def copies(count):
    return pltpu.SemaphoreType.DMA((count,))


def room(dims):
    return pltpu.VMEM(dims, F32)


def call(kernel, outs, args, scalars=(), flops=0, size=4 << 20, scratch=(), name=None, specs=None, out_specs=None, **more):
    out_shape = [shape(s) if isinstance(s, tuple) else s for s in outs]
    return pl.pallas_call(
        kernel,
        out_shape=out_shape,
        in_specs=(specs or [VMEM] * len(args)) + [SMEM] * len(scalars),
        out_specs=out_specs or [VMEM] * len(outs),
        scratch_shapes=list(scratch),
        compiler_params=PARAMS,
        cost_estimate=pl.CostEstimate(flops=flops, bytes_accessed=size, transcendentals=0),
        name=name,
        **more,
    )(*args, *scalars)


def in_hbm(x):
    return pltpu.with_memory_space_constraint(x, pltpu.HBM)


def hbm(dims):
    return pltpu.HBM(dims, F32)


def regroup(x):
    return lax.all_to_all(x, "row", 0, 0, axis_index_groups=GROUPS, tiled=True)


def earlier(x):
    return lax.ppermute(x, "seg", [(i + 1, i) for i in range(7)])


def exchange(slabs):
    perms = (PERM_I0, PERM_J1, PERM_J0, PERM_I2, PERM_CORNER)
    return [lax.ppermute(s, "row", perm) for s, perm in zip(slabs, perms)]


def body(
    terminal_adjoint,
    midpoint_state,
    controls,
    detuning,
    anharmonicity,
    decay_rate,
    dephasing,
    cross_kerr,
):
    amp = controls[0]
    dec = decay_rate[None]
    roots = jnp.asarray(ROOTS)[None]
    full = (amp, detuning[None], anharmonicity[None], dec, dephasing[None], cross_kerr[None], roots)
    few = (amp, dec, roots)
    terminal = terminal_adjoint[0]
    (packed,) = call(
        pack_kernel,
        [hbm(PACKED_SHAPE)],
        [in_hbm(terminal)],
        specs=[ANY],
        out_specs=[ANY],
        scratch=[room(PLAIN_SHAPE), room(PACKED_SHAPE), copies(8)],
        name="pack_blocks",
    )
    base = regroup(packed).reshape(UNIT_SHAPE)
    (state,) = call(deal_kernel, [STATE_SHAPE], [midpoint_state[0, 0]], name="deal_state")
    slabs = call(
        slab_kernel, slab_shapes(0), [base, state], name="slabs"
    )
    current = base
    for n in range(3):
        scale = STEP if n == 2 else 0.5 * STEP
        before = halos[1:4] if n else []
        halos = exchange(slabs)
        results = call(
            lambda *refs, n=n, scale=scale: local_kernel(scale, n, *refs),
            [UNIT_SHAPE] + [[], [STATE_SHAPE], [hbm(UNIT_SHAPE), hbm(STATE_SHAPE)]][n],
            [current, base] + ([state, *before] if n else []),
            full,
            flops=30 << 20,
            size=6 << 20,
            out_specs=[VMEM] + [[], [VMEM], [ANY, ANY]][n],
            scratch=[room(STATE_SHAPE), copies(2)] if n == 2 else [],
            name="local_terms",
        )
        part = results[0]
        if n:
            *middle, state = results[1:]
        if n < 2:
            current, *slabs = call(
                lambda *refs, n=n, scale=scale: edge_kernel(scale, n + 1, *refs),
                [UNIT_SHAPE, *slab_shapes(n + 1)],
                [part, *halos, state],
                few,
                flops=5 << 20,
                size=8 << 20,
                name="edge_terms",
            )
    final, rest = call(
        lambda *refs: edge_kernel(STEP, None, *refs),
        [hbm(BLOCKS_SHAPE), REST_SHAPE],
        [part, *halos],
        few,
        flops=5 << 20,
        size=6 << 20,
        out_specs=[ANY, VMEM],
        scratch=[room(BLOCKS_SHAPE), copies(4)],
        name="edge_terms",
    )
    here = regroup(final)
    rest_next = earlier(rest)
    (grad,) = call(
        gradient_kernel,
        [(8, WIDTH)],
        [*middle, halos[0], state, *halos[1:4]],
        (roots,),
        flops=30 << 20,
        size=6 << 20,
        specs=[ANY, VMEM, ANY, VMEM, VMEM, VMEM],
        scratch=[room(UNIT_SHAPE), room(STATE_SHAPE), room(STATE_SHAPE), copies(2)],
        name="gradient",
    )
    (joined,) = call(
        join_kernel,
        [hbm(JOINED_SHAPE)],
        [rest_next, grad],
        out_specs=[ANY],
        scratch=[copies(9)],
        name="join_blocks",
    )
    here, joined = lax.optimization_barrier((here, joined))
    rest_here = regroup(joined)
    most_next = earlier(here[:, : 16 * MOST])
    (start,) = call(
        start_kernel,
        [hbm(PLAIN_SHAPE)],
        [here],
        specs=[ANY],
        out_specs=[ANY],
        scratch=[room(BLOCKS_SHAPE), room(PLAIN_SHAPE), copies(8)],
        name="start_rows",
    )
    start, rest_here, most_next = lax.optimization_barrier((start, rest_here, most_next))
    (defect,) = call(
        finish_kernel,
        [hbm(PLAIN_SHAPE)],
        [most_next, rest_here, terminal],
        specs=[ANY] * 3,
        out_specs=[ANY],
        scratch=[room(MOST_SHAPE), room(REST_SHAPE), room(PLAIN_SHAPE), room(PLAIN_SHAPE), copies(10)],
        name="defect_rows",
    )
    grad = jnp.sum(rest_here[:, 16 * (8 - MOST) :], axis=0)
    grad = grad + lax.ppermute(grad, "row", PERM_I0)
    totals = jnp.sum(grad.reshape(8, 4, LANES), axis=(0, 2)) / ORDER
    return start[None], defect[None], totals[None, None]


def solution(mesh):
    return jax.shard_map(
        body,
        mesh=mesh,
        in_specs=(
            P("seg", None, "row", None),
            P("seg", None, None, "row", None),
            P("seg", None, None),
            P(),
            P(),
            P(),
            P(),
            P(),
        ),
        out_specs=(P("seg", None, "row", None), P("seg", None, "row", None), P("seg", None, None)),
        check_vma=False,
    )
```

```python
import jax
import jax.numpy as jnp
import numpy as np
from jax import lax
from jax.experimental import pallas as pl
from jax.experimental.pallas import tpu as pltpu
from jax.sharding import PartitionSpec as P


ORDER = 2048
STEP = 0.01
UNITS = 32
ROWS = 16
LANES = 128
TILES = 4
WIDTH = TILES * LANES
F32 = jnp.float32

GROUPS = [
    [4 * y + z for y in (0, 1) for z in (0, 1, 3, 2)],
    [4 * y + z for y in (3, 2) for z in (2, 3, 1, 0)],
]
Y_OUTER = {0: 3, 3: 0, 1: 2, 2: 1}
Y_INNER = {0: 1, 1: 0, 2: 3, 3: 2}


def pairs_y(flip):
    return [(4 * y + z, 4 * flip[y] + z) for y in range(4) for z in range(4)]


def pairs_z(flip):
    return [(4 * y + z, 4 * y + flip[z]) for y in range(4) for z in range(4)]


PERM_I0 = pairs_y(Y_OUTER)
PERM_I2 = pairs_y(Y_INNER)
PERM_J0 = pairs_z(Y_OUTER)
PERM_J1 = pairs_z(Y_INNER)
PERM_CORNER = [(4 * y + z, 4 * Y_OUTER[y] + Y_OUTER[z]) for y in (0, 1) for z in (0, 1)]
ROOTS = np.sqrt(np.arange(16)).astype(np.float32)


class Place:
    def __init__(self):
        row = lax.axis_index("row")
        y = row >> 2
        z = row & 3
        self.upper = y >> 1
        self.gi2 = jnp.where((y == 1) | (y == 2), 1, 0)
        self.gj0 = z >> 1
        self.gj1 = jnp.where((z == 1) | (z == 2), 1, 0)


def unit_at(p, i1):
    odd = p & 1
    return ((p >> 1) << 4) + (((i1 >> 2) ^ (3 * odd)) << 2) + (i1 & 3)


def wide(unit):
    return unit + ((unit >> 2) << 2)


def iotas():
    lane = lax.broadcasted_iota(jnp.int32, (ROWS, LANES), 1)
    sub = lax.broadcasted_iota(jnp.int32, (ROWS, LANES), 0)
    return lane, sub


class Tables:
    def __init__(self, place):
        lane, sub = iotas()
        low1 = lane >> 5
        self.j1 = (low1 + 4 * place.gj1).astype(F32)
        self.j2 = ((lane >> 2) & 7).astype(F32)
        self.j3 = (lane & 3).astype(F32)
        low2 = sub >> 2
        self.i2 = (low2 + 4 * place.gi2).astype(F32)
        self.i3 = (sub & 3).astype(F32)
        self.c1p = jnp.where(low1 > 0, jnp.sqrt(self.j1), 0.0)
        self.c1m = jnp.where(low1 < 3, jnp.sqrt(self.j1 + 1.0), 0.0)
        self.c2p = jnp.sqrt(self.j2)
        self.c2m = jnp.where(self.j2 < 7.0, jnp.sqrt(self.j2 + 1.0), 0.0)
        self.c3p = jnp.sqrt(self.j3)
        self.c3m = jnp.where(self.j3 < 3.0, jnp.sqrt(self.j3 + 1.0), 0.0)
        self.r2p = jnp.where(low2 > 0, jnp.sqrt(self.i2), 0.0)
        self.r2m = jnp.where(low2 < 3, jnp.sqrt(self.i2 + 1.0), 0.0)
        self.r3p = jnp.sqrt(self.i3)
        self.r3m = jnp.where(self.i3 < 3.0, jnp.sqrt(self.i3 + 1.0), 0.0)
        edge1 = jnp.where(place.gj1 == 1, 0, 3)
        edge2 = jnp.where(place.gi2 == 1, 0, 3)
        self.edge1 = edge1
        self.at1 = (low1 == edge1).astype(F32)
        self.at2 = (low2 == edge2).astype(F32)


def drift(levels, detuning, anharmonicity, cross_kerr):
    total = 0.0
    for q in range(4):
        n = levels[q]
        total = total + detuning[q] * n - 0.5 * anharmonicity[q] * n * (n - 1.0)
    k = 0
    for a in range(4):
        for b in range(a + 1, 4):
            total = total - cross_kerr[k] * levels[a] * levels[b]
            k += 1
    return total


def decay_part(levels, decay, dephasing):
    total = 0.0
    for q in range(4):
        n = levels[q]
        total = total - 0.5 * decay[q] * n - 0.5 * dephasing[q] * n * n
    return total


def tile(ref, unit, c, t):
    return ref[unit, c, :, t * LANES : (t + 1) * LANES]


def level_of(place, p):
    return jnp.where(place.upper == 1, 7 - p, p)


def unit_neighbours(place, roots, p, i1, at=unit_at):
    up = place.upper == 1
    i0 = level_of(place, p)
    below = jnp.where(up, p + 1, p - 1)
    above = jnp.where(up, p - 1, p + 1)
    root_below = jnp.where((below >= 0) & (below <= 3), roots[0, i0], 0.0)
    root_above = jnp.where((above >= 0) & (above <= 3), roots[0, i0 + 1], 0.0)
    return (
        i0,
        (at(jnp.clip(below, 0, 3), i1), root_below),
        (at(jnp.clip(above, 0, 3), i1), root_above),
        (at(p, jnp.maximum(i1 - 1, 0)), roots[0, i1]),
        (at(p, jnp.minimum(i1 + 1, 7)), jnp.where(i1 < 7, roots[0, i1 + 1], 0.0)),
    )


def local_kernel(scale, n, *refs):
    z, base, *scalars, out = refs[:10]
    writes = []
    if n == 2:
        z_out, sems = refs[10:]
        writes = [pltpu.make_async_copy(z, z_out, sems.at[0])]
    start_all(writes)
    amp, det, anh, dec, dep, kerr, roots = scalars
    def at(p, i1):
        return unit_at(p, i1) if n else wide(unit_at(p, i1))

    place = Place()
    tb = Tables(place)
    detuning = [det[0, q] for q in range(4)]
    anharm = [anh[0, q] for q in range(4)]
    decay = [dec[0, q] for q in range(4)]
    dephasing = [dep[0, q] for q in range(4)]
    cross = [kerr[0, k] for k in range(6)]
    u = [amp[0, q] for q in range(4)]
    column_energy = []
    column_decay = []
    for t in range(TILES):
        j0 = (4 * place.gj0 + t).astype(F32)
        levels = [j0, tb.j1, tb.j2, tb.j3]
        column_energy.append(drift(levels, detuning, anharm, cross))
        column_decay.append(decay_part(levels, decay, dephasing))
    cross2 = dephasing[2] * tb.i2
    cross3 = dephasing[3] * tb.i3
    c1m, c2m, c3m = u[1] * tb.c1m, u[2] * tb.c2m, u[3] * tb.c3m
    c1p, c2p, c3p = u[1] * tb.c1p, u[2] * tb.c2p, u[3] * tb.c3p
    r2m, r3m = u[2] * tb.r2m, u[3] * tb.r3m
    r2p, r3p = u[2] * tb.r2p, u[3] * tb.r3p
    d2p, d3p = decay[2] * tb.r2p, decay[3] * tb.r3p

    def step(unit, carry):
        p = unit >> 3
        i1 = unit & 7
        here = unit_at(p, i1)
        mine = at(p, i1)
        i0, below, above, less, more = unit_neighbours(place, roots, p, i1, at)
        i0f = i0.astype(F32)
        i1f = i1.astype(F32)
        rows = [i0f, i1f, tb.i2, tb.i3]
        row_energy = drift(rows, detuning, anharm, cross)
        row_decay = decay_part(rows, decay, dephasing)
        d1p = (decay[1] * less[1]) * tb.c1p
        for t in range(TILES):
            j0 = 4 * place.gj0 + t
            root_left = roots[0, j0]
            root_right = roots[0, j0 + 1]
            comm = []
            sand = []
            values = []
            for c in range(2):
                m = tile(z, mine, c, t)
                values.append(m)
                turned2 = pltpu.roll(m, 4, 1)
                turned3 = pltpu.roll(m, 1, 1)
                row1 = tile(z, less[0], c, t)
                row0 = tile(z, below[0], c, t)
                k = (u[0] * below[1]) * row0 + (u[0] * above[1]) * tile(z, above[0], c, t)
                k = k + (u[1] * less[1]) * row1 + (u[1] * more[1]) * tile(z, more[0], c, t)
                if t > 0:
                    k = k - (u[0] * root_left) * tile(z, mine, c, t - 1)
                if t < TILES - 1:
                    k = k - (u[0] * root_right) * tile(z, mine, c, t + 1)
                k = k + r2p * pltpu.roll(m, 4, 0) + r2m * pltpu.roll(m, ROWS - 4, 0)
                k = k + r3p * pltpu.roll(m, 1, 0) + r3m * pltpu.roll(m, ROWS - 1, 0)
                k = k - c1p * pltpu.roll(m, 32, 1) - c1m * pltpu.roll(m, LANES - 32, 1)
                k = k - c2p * turned2 - c2m * pltpu.roll(m, LANES - 4, 1)
                k = k - c3p * turned3 - c3m * pltpu.roll(m, LANES - 1, 1)
                comm.append(k)
                s = (
                    d1p * pltpu.roll(row1, 32, 1)
                    + d2p * pltpu.roll(tb.c2p * turned2, 4, 0)
                    + d3p * pltpu.roll(tb.c3p * turned3, 1, 0)
                )
                if t > 0:
                    s = s + (decay[0] * below[1] * root_left) * tile(z, below[0], c, t - 1)
                sand.append(s)
            phase = row_energy - column_energy[t]
            damping = (
                row_decay
                + (column_decay[t] + (dephasing[0] * i0f) * j0.astype(F32))
                + (dephasing[1] * i1f) * tb.j1
                + cross2 * tb.j2
                + cross3 * tb.j3
            )
            x, y = values
            lanes = slice(t * LANES, (t + 1) * LANES)
            out[here, 0, :, lanes] = tile(base, wide(here), 0, t) + scale * (
                damping * x - phase * y - comm[1] + sand[0]
            )
            out[here, 1, :, lanes] = tile(base, wide(here), 1, t) + scale * (
                damping * y + phase * x + comm[0] + sand[1]
            )
        return carry

    lax.fori_loop(0, UNITS, step, 0)
    wait_all(writes)


def start_all(copies):
    for copy in copies:
        copy.start()


def wait_all(copies):
    for copy in copies:
        copy.wait()


def put_slabs(place, tb, p, pair, both, s_i0, s_j1, s_j0, s_i2, s_c):
    lane, _ = iotas()
    half = lax.broadcasted_iota(jnp.int32, (8, LANES), 0) < 4
    block = lane >> 5
    gj0 = place.gj0 == 1
    gi2 = place.gi2 == 1
    for par in range(2):
        i1 = 2 * pair + par
        n = p * 8 + i1
        for c in range(2):
            tiles = both[par][c]
            if p == 3:
                for t in range(TILES):
                    s_i0[i1, c, :, t * LANES : (t + 1) * LANES] = tiles[t]
                s_c[i1, c] = tiles[TILES - 1]
            s_j0[2 * n + c] = jnp.where(gj0, tiles[0], tiles[TILES - 1])
            packed = None
            for t in range(TILES):
                turned = pltpu.roll(tiles[t], (32 * (t - tb.edge1)) & (LANES - 1), 1)
                packed = turned if packed is None else jnp.where(block == t, turned, packed)
            s_j1[2 * n + c] = packed
    for c in range(2):
        for t in range(TILES):
            even, odd = both[0][c][t], both[1][c][t]
            first = jnp.where(gi2, even[0:8], pltpu.roll(even[8:16], 4, 0))
            second = jnp.where(gi2, pltpu.roll(odd[0:8], 4, 0), odd[8:16])
            entry = ((p * 4 + pair) * 2 + c) * 2 + t // 2
            s_i2[entry, (t % 2) * 8 : (t % 2) * 8 + 8] = jnp.where(half, first, second)


def slab_kernel(z, s_i0, s_j1, s_j0, s_i2, s_c):
    place = Place()
    tb = Tables(place)
    for p in range(4):

        def step(pair, carry, p=p):
            both = [
                [[tile(z, wide(unit_at(p, 2 * pair + par)), c, t) for t in range(TILES)] for c in range(2)]
                for par in range(2)
            ]
            put_slabs(place, tb, p, pair, both, s_i0, s_j1, s_j0, s_i2, s_c)
            return carry

        lax.fori_loop(0, 4, step, 0)


def i2_halo(place, h_i2, p, pair, par, c, t):
    small = h_i2[((p * 4 + pair) * 2 + c) * 2 + t // 2, (t % 2) * 8 : (t % 2) * 8 + 8]
    small = pltpu.roll(small, 4 * ((par + 1 + place.gi2) & 1), 0)
    return jnp.concatenate([small, small], axis=0)


def edge_kernel(scale, last, *refs):
    part, h_i0, h_j1, h_j0, h_i2, h_c = refs[:6]
    if last:
        amp, dec, roots, out_all, out_rest, block, sems = refs[6:]
        later = 16 * MOST
    else:
        amp, dec, roots, out, *slabs = refs[6:]
    place = Place()
    tb = Tables(place)
    up = place.upper == 1
    upf = place.upper.astype(F32)
    gj0f = place.gj0.astype(F32)
    gj1f = place.gj1.astype(F32)
    gi2f = place.gi2.astype(F32)
    copies = []
    decay = [scale * dec[0, q] for q in range(4)]
    u = [scale * amp[0, q] for q in range(4)]
    s1_base = (decay[1] * 2.0 * gj1f) * tb.at1
    s2_base = (decay[2] * 2.0 * gi2f) * tb.at2 * tb.c2p
    k1_mask = (-2.0 * u[1]) * tb.at1
    k2_mask = (2.0 * u[2]) * tb.at2

    def one(p, pair, par):
        i0 = jnp.where(up, 7 - p, p)
        below = jnp.where(up, p + 1, p - 1)
        below_in = (below >= 0) & (below <= 3)
        below = jnp.clip(below, 0, 3)
        root_below = jnp.where(below_in, roots[0, i0], 0.0)
        i1 = 2 * pair + par
        here = unit_at(p, i1)
        n = p * 8 + i1
        s1_less = roots[0, i1] * s1_base
        n_less = p * 8 + jnp.maximum(i1 - 1, 0)
        new = [[], []]
        for t in range(TILES):
            j0 = 4 * place.gj0 + t
            lanes = slice(t * LANES, (t + 1) * LANES)
            turn = (32 * (tb.edge1 - t)) & (LANES - 1)
            comm = []
            sand = []
            for c in range(2):
                across = i2_halo(place, h_i2, p, pair, par, c, t)
                k = k2_mask * across + k1_mask * pltpu.roll(h_j1[2 * n + c], turn, 1)
                s = s2_base * pltpu.roll(across, 4, 1) + s1_less * pltpu.roll(h_j1[2 * n_less + c], turn, 1)
                if p == 3:
                    k = k + (2.0 * u[0]) * h_i0[i1, c, :, lanes]
                    if t > 0:
                        s = s + (decay[0] * 2.0 * upf * roots[0, j0]) * h_i0[
                            i1, c, :, (t - 1) * LANES : t * LANES
                        ]
                    else:
                        s = s + (decay[0] * 4.0 * upf * gj0f) * h_c[i1, c]
                if t == 0 or t == TILES - 1:
                    on = gj0f if t == 0 else 1.0 - gj0f
                    k = k - (2.0 * u[0] * on) * h_j0[2 * n + c]
                if t == 0:
                    s = s + (decay[0] * 2.0 * gj0f * root_below) * h_j0[2 * (below * 8 + i1) + c]
                comm.append(k)
                sand.append(s)
            new[0].append(tile(part, here, 0, t) + (sand[0] - comm[1]))
            new[1].append(tile(part, here, 1, t) + (sand[1] + comm[0]))
        return here, new

    for p in range(4):

        def step(pair, carry, p=p):
            both = []
            for par in range(2):
                here, new = one(p, pair, par)
                for c in range(2):
                    for t in range(TILES):
                        out[here, c, :, t * LANES : (t + 1) * LANES] = new[c][t]
                both.append(new)
            put_slabs(place, tb, p, pair, both, *slabs)
            return carry

        def last_step(h, carry, p=p):
            for a in range(4):
                here, new = one(p, 2 * h + a // 2, a % 2)
                for c in range(2):
                    for t in range(TILES):
                        lanes = slice(t * LANES, (t + 1) * LANES)
                        at = (2 * a + c) * ROWS
                        block[here >> 2, at : at + ROWS, lanes] = new[c][t]
            return carry

        if last:
            lax.fori_loop(0, 2, last_step, 0)
            slots = pl.ds(2 * p, 2)
            rows = pl.ds(later, 128 - later)
            copies.append(pltpu.make_async_copy(block.at[slots], out_all.at[slots], sems.at[p]))
            copies.append(pltpu.make_async_copy(block.at[slots, rows], out_rest.at[slots], sems.at[4 + p]))
            start_all(copies[-2:])
        else:
            lax.fori_loop(0, 4, step, 0)
    wait_all(copies)


def gradient_kernel(z_in, rho_in, h_i0, h_j1, h_j0, h_i2, roots, grad, z, rho, sems):
    reads = [pltpu.make_async_copy(rho_in.at[:, pl.ds(4, 4)], rho, sems.at[0]), pltpu.make_async_copy(z_in, z, sems.at[1])]
    start_all(reads)
    place = Place()
    tb = Tables(place)
    gj0f = place.gj0.astype(F32)
    wait_all(reads)
    k1_mask = -2.0 * tb.at1
    k2_mask = 2.0 * tb.at2

    def half_step(n, par, acc):
        p = n >> 2
        pair = n & 3
        i1 = 2 * pair + par
        unit = p * 8 + i1
        here = unit_at(p, i1)
        _, below, above, less, more = unit_neighbours(place, roots, p, i1)
        outer = jnp.where(p == 3, 2.0, 0.0)
        for t in range(TILES):
            j0 = 4 * place.gj0 + t
            turn = (32 * (tb.edge1 - t)) & (LANES - 1)
            for c in range(2):
                m = tile(z, here, c, t)
                k0 = below[1] * tile(z, below[0], c, t) + above[1] * tile(z, above[0], c, t)
                k0 = k0 + outer * h_i0[i1, c, :, t * LANES : (t + 1) * LANES]
                if t > 0:
                    k0 = k0 - roots[0, j0] * tile(z, here, c, t - 1)
                if t < TILES - 1:
                    k0 = k0 - roots[0, j0 + 1] * tile(z, here, c, t + 1)
                if t == 0 or t == TILES - 1:
                    on = gj0f if t == 0 else 1.0 - gj0f
                    k0 = k0 - (2.0 * on) * h_j0[2 * unit + c]
                k1 = less[1] * tile(z, less[0], c, t) + more[1] * tile(z, more[0], c, t)
                k1 = k1 - tb.c1p * pltpu.roll(m, 32, 1) - tb.c1m * pltpu.roll(m, LANES - 32, 1)
                k1 = k1 + k1_mask * pltpu.roll(h_j1[2 * unit + c], turn, 1)
                k2 = tb.r2p * pltpu.roll(m, 4, 0) + tb.r2m * pltpu.roll(m, ROWS - 4, 0)
                k2 = k2 - tb.c2p * pltpu.roll(m, 4, 1) - tb.c2m * pltpu.roll(m, LANES - 4, 1)
                k2 = k2 + k2_mask * i2_halo(place, h_i2, p, pair, par, c, t)
                k3 = tb.r3p * pltpu.roll(m, 1, 0) + tb.r3m * pltpu.roll(m, ROWS - 1, 0)
                k3 = k3 - tb.c3p * pltpu.roll(m, 1, 1) - tb.c3m * pltpu.roll(m, LANES - 1, 1)
                other = rho[here >> 2, here & 3, 1 - c, :, t * LANES : (t + 1) * LANES]
                if c == 1:
                    other = -other
                acc = [acc[q] + k * other for q, k in enumerate((k0, k1, k2, k3))]
        return acc

    def step(n, carry):
        acc = list(carry)
        for par in range(2):
            acc = half_step(n, par, acc)
        return tuple(acc)

    total = lax.fori_loop(0, UNITS // 2, step, tuple(jnp.zeros((ROWS, LANES), F32) for _ in range(4)))
    for q in range(4):
        grad[:, q * LANES : (q + 1) * LANES] = total[q][0:8] + total[q][8:16]


def chunk_lanes(g, t):
    start = (g // 2) * 1024 + t * 256 + (g % 2) * 128
    return slice(start, start + LANES)


def slice_rows(a):
    return pl.ds(32 * a, 32)


def pack_kernel(adjoint, state, out, plain, block, sems):
    upper = lax.axis_index("row") >> 3
    reads = []
    for m, x in enumerate((adjoint, state)):
        for a in range(4):
            rows = slice_rows(a)
            reads.append(pltpu.make_async_copy(x.at[:, rows], plain.at[m, :, rows], sems.at[4 * m + a]))
    writes = [pltpu.make_async_copy(block.at[:, at], out.at[:, at], sems.at[8 + at]) for at in range(8)]
    start_all(reads)
    for at in range(8):
        m, a = at // 4, at % 4
        reads[at].wait()
        for gi2 in range(2):
            for g in range(4):
                k = 4 * gi2 + jnp.where(upper == 1, 3 - g, g)
                for c in range(2):
                    for t in range(TILES):
                        block[k, at, c, :, t * LANES : (t + 1) * LANES] = plain[
                            m, c, 32 * a + 16 * gi2 : 32 * a + 16 * gi2 + 16, chunk_lanes(g, t)
                        ]
        writes[at].start()
    wait_all(writes)


def join_kernel(blocks, grad, out, sems):
    rows = 16 * (8 - MOST)
    copies = [pltpu.make_async_copy(blocks, out.at[:, pl.ds(0, rows)], sems.at[8])]
    for k in range(8):
        copies.append(pltpu.make_async_copy(grad, out.at[k, pl.ds(rows, 8)], sems.at[k]))
    start_all(copies)
    wait_all(copies)


def undeal(upper, index, source, first, out, base=None):
    a, c = index // 2, index % 2
    for gi2 in range(2):
        rows = slice(32 * a + 16 * gi2, 32 * a + 16 * gi2 + 16)
        for g in range(4):
            k = 4 * gi2 + jnp.where(upper == 1, 3 - g, g)
            for t in range(TILES):
                lanes = chunk_lanes(g, t)
                value = source[k, first : first + 16, t * LANES : (t + 1) * LANES]
                if base is not None:
                    value = base[c, rows, lanes] - value
                out[c, rows, lanes] = value


def start_kernel(blocks, start, held, plain, sems):
    upper = lax.axis_index("row") >> 3
    reads = [
        pltpu.make_async_copy(blocks.at[:, pl.ds(32 * a, 32)], held.at[:, pl.ds(32 * a, 32)], sems.at[a])
        for a in range(4)
    ]
    writes = [
        pltpu.make_async_copy(plain.at[:, slice_rows(a)], start.at[:, slice_rows(a)], sems.at[4 + a])
        for a in range(4)
    ]
    start_all(reads)
    for a in range(4):
        reads[a].wait()
        for c in range(2):
            undeal(upper, 2 * a + c, held, 32 * a + 16 * c, plain)
        writes[a].start()
    wait_all(writes)


def finish_kernel(most, rest, base, defect, held_most, held_rest, held_base, plain, sems):
    upper = lax.axis_index("row") >> 3
    rows = 16 * (8 - MOST)
    reads = [
        pltpu.make_async_copy(rest.at[:, pl.ds(0, rows)], held_rest, sems.at[0]),
        pltpu.make_async_copy(most, held_most, sems.at[1]),
    ]
    order = (3, 2, 1, 0)
    for a in order:
        reads.append(
            pltpu.make_async_copy(base.at[:, slice_rows(a)], held_base.at[:, slice_rows(a)], sems.at[2 + a])
        )
    writes = [
        pltpu.make_async_copy(plain.at[:, slice_rows(a)], defect.at[:, slice_rows(a)], sems.at[6 + a])
        for a in order
    ]
    start_all(reads)
    reads[0].wait()
    for at, a in enumerate(order):
        if at == 1:
            reads[1].wait()
        reads[2 + at].wait()
        for c in range(2):
            index = 2 * a + c
            if index < MOST:
                undeal(upper, index, held_most, 16 * index, plain, held_base)
            else:
                undeal(upper, index, held_rest, 16 * (index - MOST), plain, held_base)
        writes[at].start()
    wait_all(writes)


VMEM = pl.BlockSpec(memory_space=pltpu.VMEM)
SMEM = pl.BlockSpec(memory_space=pltpu.SMEM)
ANY = pl.BlockSpec(memory_space=pl.ANY)
PARAMS = pltpu.CompilerParams(vmem_limit_bytes=16 * 1024 * 1024)
MOST = 5
UNIT_SHAPE = (UNITS, 2, ROWS, WIDTH)
PACKED_SHAPE = (8, 8, 2, ROWS, WIDTH)
PLAIN_SHAPE = (2, 128, ORDER)
BLOCKS_SHAPE = (8, 128, WIDTH)
MOST_SHAPE = (8, 16 * MOST, WIDTH)
REST_SHAPE = (8, 16 * (8 - MOST), WIDTH)
JOINED_SHAPE = (8, 16 * (8 - MOST) + 8, WIDTH)


SLAB_SHAPES = [(8, 2, ROWS, WIDTH)] + [(64, ROWS, LANES)] * 3 + [(8, 2, ROWS, LANES)]


def shape(dims):
    return jax.ShapeDtypeStruct(dims, F32)


def copies(count):
    return pltpu.SemaphoreType.DMA((count,))


def room(dims):
    return pltpu.VMEM(dims, F32)


def call(kernel, outs, args, scalars=(), flops=0, size=4 << 20, scratch=(), name=None, specs=None, out_specs=None, **more):
    out_shape = [shape(s) if isinstance(s, tuple) else s for s in outs]
    return pl.pallas_call(
        kernel,
        out_shape=out_shape,
        in_specs=(specs or [VMEM] * len(args)) + [SMEM] * len(scalars),
        out_specs=out_specs or [VMEM] * len(outs),
        scratch_shapes=list(scratch),
        compiler_params=PARAMS,
        cost_estimate=pl.CostEstimate(flops=flops, bytes_accessed=size, transcendentals=0),
        name=name,
        **more,
    )(*args, *scalars)


def in_hbm(x):
    return pltpu.with_memory_space_constraint(x, pltpu.HBM)


def hbm(dims):
    return pltpu.HBM(dims, F32)


def pack(adjoint, state):
    (packed,) = call(
        pack_kernel,
        [hbm(PACKED_SHAPE)],
        [in_hbm(adjoint), in_hbm(state)],
        specs=[ANY, ANY],
        out_specs=[ANY],
        scratch=[room((2, *PLAIN_SHAPE)), room(PACKED_SHAPE), copies(16)],
        name="pack_blocks",
    )
    return packed


def regroup(x):
    return lax.all_to_all(x, "row", 0, 0, axis_index_groups=GROUPS, tiled=True)


def earlier(x):
    return lax.ppermute(x, "seg", [(i + 1, i) for i in range(7)])


def exchange(slabs, perms):
    return [lax.ppermute(s, "row", perm) for s, perm in zip(slabs, perms)]


def body(
    terminal_adjoint,
    midpoint_state,
    controls,
    detuning,
    anharmonicity,
    decay_rate,
    dephasing,
    cross_kerr,
):
    amp = controls[0]
    dec = decay_rate[None]
    roots = jnp.asarray(ROOTS)[None]
    full = (amp, detuning[None], anharmonicity[None], dec, dephasing[None], cross_kerr[None], roots)
    few = (amp, dec, roots)
    terminal = terminal_adjoint[0]
    both = regroup(pack(terminal, midpoint_state[0, 0]))
    base = both.reshape(2 * UNITS, 2, ROWS, WIDTH)
    slabs = call(slab_kernel, SLAB_SHAPES, [base], name="slabs")
    current = base
    for n in range(3):
        scale = STEP if n == 2 else 0.5 * STEP
        halos = exchange(slabs, (PERM_I0, PERM_J1, PERM_J0, PERM_I2, PERM_CORNER))
        part, *middle = call(
            lambda *refs, n=n, scale=scale: local_kernel(scale, n, *refs),
            [UNIT_SHAPE] + [hbm(UNIT_SHAPE)] * (n == 2),
            [current, base],
            full,
            flops=30 << 20,
            size=6 << 20,
            out_specs=[VMEM] + [ANY] * (n == 2),
            scratch=[copies(1)] if n == 2 else [],
            name="local_terms",
        )
        if n < 2:
            current, *slabs = call(
                lambda *refs, scale=scale: edge_kernel(scale, False, *refs),
                [UNIT_SHAPE, *SLAB_SHAPES],
                [part, *halos],
                few,
                flops=5 << 20,
                size=8 << 20,
                name="edge_terms",
            )
    final, rest = call(
        lambda *refs: edge_kernel(STEP, True, *refs),
        [hbm(BLOCKS_SHAPE), hbm(REST_SHAPE)],
        [part, *halos],
        few,
        flops=5 << 20,
        size=6 << 20,
        out_specs=[ANY, ANY],
        scratch=[room(BLOCKS_SHAPE), copies(8)],
        name="edge_terms",
    )
    here = regroup(final)
    rest_next = earlier(rest)
    (grad,) = call(
        gradient_kernel,
        [(8, WIDTH)],
        [*middle, both, *halos[:4]],
        (roots,),
        flops=30 << 20,
        size=6 << 20,
        specs=[ANY] * 2 + [VMEM] * 4,
        scratch=[room(UNIT_SHAPE), room((8, 4, 2, ROWS, WIDTH)), copies(2)],
        name="gradient",
    )
    grad = grad + lax.ppermute(grad, "row", PERM_I0)
    (joined,) = call(
        join_kernel,
        [hbm(JOINED_SHAPE)],
        [rest_next, grad],
        out_specs=[ANY],
        scratch=[copies(9)],
        name="join_blocks",
    )
    here, joined = lax.optimization_barrier((here, joined))
    rest_here = regroup(joined)
    most_next = earlier(here[:, : 16 * MOST])
    (start,) = call(
        start_kernel,
        [hbm(PLAIN_SHAPE)],
        [here],
        specs=[ANY],
        out_specs=[ANY],
        scratch=[room(BLOCKS_SHAPE), room(PLAIN_SHAPE), copies(8)],
        name="start_rows",
    )
    start, rest_here, most_next = lax.optimization_barrier((start, rest_here, most_next))
    (defect,) = call(
        finish_kernel,
        [hbm(PLAIN_SHAPE)],
        [most_next, rest_here, in_hbm(terminal)],
        specs=[ANY] * 3,
        out_specs=[ANY],
        scratch=[room(MOST_SHAPE), room(REST_SHAPE), room(PLAIN_SHAPE), room(PLAIN_SHAPE), copies(10)],
        name="defect_rows",
    )
    sums = rest_here[:, 16 * (8 - MOST) :].reshape(8, 8, 4, LANES)
    totals = jnp.sum(sums, axis=(0, 1, 3)) / ORDER
    return start[None], defect[None], totals[None, None]


def solution(mesh):
    return jax.shard_map(
        body,
        mesh=mesh,
        in_specs=(
            P("seg", None, "row", None),
            P("seg", None, None, "row", None),
            P("seg", None, None),
            P(),
            P(),
            P(),
            P(),
            P(),
        ),
        out_specs=(P("seg", None, "row", None), P("seg", None, "row", None), P("seg", None, None)),
        check_vma=False,
    )
```

```python
import jax
import jax.numpy as jnp
import numpy as np
from jax import lax
from jax.experimental import pallas as pl
from jax.experimental.pallas import tpu as pltpu
from jax.sharding import PartitionSpec as P


ORDER = 2048
STEP = 0.01
UNITS = 32
ROWS = 16
LANES = 128
TILES = 4
WIDTH = TILES * LANES
F32 = jnp.float32

GROUPS = [
    [4 * y + z for y in (0, 1) for z in (0, 1, 3, 2)],
    [4 * y + z for y in (3, 2) for z in (2, 3, 1, 0)],
]
Y_OUTER = {0: 3, 3: 0, 1: 2, 2: 1}
Y_INNER = {0: 1, 1: 0, 2: 3, 3: 2}


def pairs_y(flip):
    return [(4 * y + z, 4 * flip[y] + z) for y in range(4) for z in range(4)]


def pairs_z(flip):
    return [(4 * y + z, 4 * y + flip[z]) for y in range(4) for z in range(4)]


PERM_I0 = pairs_y(Y_OUTER)
PERM_I2 = pairs_y(Y_INNER)
PERM_J0 = pairs_z(Y_OUTER)
PERM_J1 = pairs_z(Y_INNER)
PERM_CORNER = [(4 * y + z, 4 * Y_OUTER[y] + Y_OUTER[z]) for y in (0, 1) for z in (0, 1)]
ROOTS = np.sqrt(np.arange(16)).astype(np.float32)


class Place:
    def __init__(self):
        row = lax.axis_index("row")
        y = row >> 2
        z = row & 3
        self.upper = y >> 1
        self.gi2 = jnp.where((y == 1) | (y == 2), 1, 0)
        self.gj0 = z >> 1
        self.gj1 = jnp.where((z == 1) | (z == 2), 1, 0)


def unit_at(p, i1):
    odd = p & 1
    return ((p >> 1) << 4) + (((i1 >> 2) ^ (3 * odd)) << 2) + (i1 & 3)


def wide(unit):
    return unit + ((unit >> 2) << 2)


def iotas():
    lane = lax.broadcasted_iota(jnp.int32, (ROWS, LANES), 1)
    sub = lax.broadcasted_iota(jnp.int32, (ROWS, LANES), 0)
    return lane, sub


class Tables:
    def __init__(self, place):
        lane, sub = iotas()
        low1 = lane >> 5
        self.j1 = (low1 + 4 * place.gj1).astype(F32)
        self.j2 = ((lane >> 2) & 7).astype(F32)
        self.j3 = (lane & 3).astype(F32)
        low2 = sub >> 2
        self.i2 = (low2 + 4 * place.gi2).astype(F32)
        self.i3 = (sub & 3).astype(F32)
        self.c1p = jnp.where(low1 > 0, jnp.sqrt(self.j1), 0.0)
        self.c1m = jnp.where(low1 < 3, jnp.sqrt(self.j1 + 1.0), 0.0)
        self.c2p = jnp.sqrt(self.j2)
        self.c2m = jnp.where(self.j2 < 7.0, jnp.sqrt(self.j2 + 1.0), 0.0)
        self.c3p = jnp.sqrt(self.j3)
        self.c3m = jnp.where(self.j3 < 3.0, jnp.sqrt(self.j3 + 1.0), 0.0)
        self.r2p = jnp.where(low2 > 0, jnp.sqrt(self.i2), 0.0)
        self.r2m = jnp.where(low2 < 3, jnp.sqrt(self.i2 + 1.0), 0.0)
        self.r3p = jnp.sqrt(self.i3)
        self.r3m = jnp.where(self.i3 < 3.0, jnp.sqrt(self.i3 + 1.0), 0.0)
        edge1 = jnp.where(place.gj1 == 1, 0, 3)
        edge2 = jnp.where(place.gi2 == 1, 0, 3)
        self.edge1 = edge1
        self.at1 = (low1 == edge1).astype(F32)
        self.at2 = (low2 == edge2).astype(F32)


def drift(levels, detuning, anharmonicity, cross_kerr):
    total = 0.0
    for q in range(4):
        n = levels[q]
        total = total + detuning[q] * n - 0.5 * anharmonicity[q] * n * (n - 1.0)
    k = 0
    for a in range(4):
        for b in range(a + 1, 4):
            total = total - cross_kerr[k] * levels[a] * levels[b]
            k += 1
    return total


def decay_part(levels, decay, dephasing):
    total = 0.0
    for q in range(4):
        n = levels[q]
        total = total - 0.5 * decay[q] * n - 0.5 * dephasing[q] * n * n
    return total


def tile(ref, unit, c, t):
    return ref[unit, c, :, t * LANES : (t + 1) * LANES]


def level_of(place, p):
    return jnp.where(place.upper == 1, 7 - p, p)


def unit_neighbours(place, roots, p, i1, at=unit_at):
    up = place.upper == 1
    i0 = level_of(place, p)
    below = jnp.where(up, p + 1, p - 1)
    above = jnp.where(up, p - 1, p + 1)
    root_below = jnp.where((below >= 0) & (below <= 3), roots[0, i0], 0.0)
    root_above = jnp.where((above >= 0) & (above <= 3), roots[0, i0 + 1], 0.0)
    return (
        i0,
        (at(jnp.clip(below, 0, 3), i1), root_below),
        (at(jnp.clip(above, 0, 3), i1), root_above),
        (at(p, jnp.maximum(i1 - 1, 0)), roots[0, i1]),
        (at(p, jnp.minimum(i1 + 1, 7)), jnp.where(i1 < 7, roots[0, i1 + 1], 0.0)),
    )


def local_kernel(scale, n, *refs):
    z, base, *scalars, out = refs[:10]
    writes = []
    if n == 2:
        z_out, sems = refs[10:]
        writes = [pltpu.make_async_copy(z, z_out, sems.at[0])]
    start_all(writes)
    amp, det, anh, dec, dep, kerr, roots = scalars
    def at(p, i1):
        return unit_at(p, i1) if n else wide(unit_at(p, i1))

    place = Place()
    tb = Tables(place)
    detuning = [det[0, q] for q in range(4)]
    anharm = [anh[0, q] for q in range(4)]
    decay = [dec[0, q] for q in range(4)]
    dephasing = [dep[0, q] for q in range(4)]
    cross = [kerr[0, k] for k in range(6)]
    u = [amp[0, q] for q in range(4)]
    column_energy = []
    column_decay = []
    for t in range(TILES):
        j0 = (4 * place.gj0 + t).astype(F32)
        levels = [j0, tb.j1, tb.j2, tb.j3]
        column_energy.append(drift(levels, detuning, anharm, cross))
        column_decay.append(decay_part(levels, decay, dephasing))
    cross2 = dephasing[2] * tb.i2
    cross3 = dephasing[3] * tb.i3
    c1m, c2m, c3m = u[1] * tb.c1m, u[2] * tb.c2m, u[3] * tb.c3m
    c1p, c2p, c3p = u[1] * tb.c1p, u[2] * tb.c2p, u[3] * tb.c3p
    r2m, r3m = u[2] * tb.r2m, u[3] * tb.r3m
    r2p, r3p = u[2] * tb.r2p, u[3] * tb.r3p
    d2p, d3p = decay[2] * tb.r2p, decay[3] * tb.r3p

    def step(unit, carry):
        p = unit >> 3
        i1 = unit & 7
        here = unit_at(p, i1)
        mine = at(p, i1)
        i0, below, above, less, more = unit_neighbours(place, roots, p, i1, at)
        i0f = i0.astype(F32)
        i1f = i1.astype(F32)
        rows = [i0f, i1f, tb.i2, tb.i3]
        row_energy = drift(rows, detuning, anharm, cross)
        row_decay = decay_part(rows, decay, dephasing)
        d1p = (decay[1] * less[1]) * tb.c1p
        for t in range(TILES):
            j0 = 4 * place.gj0 + t
            root_left = roots[0, j0]
            root_right = roots[0, j0 + 1]
            comm = []
            sand = []
            values = []
            for c in range(2):
                m = tile(z, mine, c, t)
                values.append(m)
                turned2 = pltpu.roll(m, 4, 1)
                turned3 = pltpu.roll(m, 1, 1)
                row1 = tile(z, less[0], c, t)
                row0 = tile(z, below[0], c, t)
                k = (u[0] * below[1]) * row0 + (u[0] * above[1]) * tile(z, above[0], c, t)
                k = k + (u[1] * less[1]) * row1 + (u[1] * more[1]) * tile(z, more[0], c, t)
                if t > 0:
                    k = k - (u[0] * root_left) * tile(z, mine, c, t - 1)
                if t < TILES - 1:
                    k = k - (u[0] * root_right) * tile(z, mine, c, t + 1)
                k = k + r2p * pltpu.roll(m, 4, 0) + r2m * pltpu.roll(m, ROWS - 4, 0)
                k = k + r3p * pltpu.roll(m, 1, 0) + r3m * pltpu.roll(m, ROWS - 1, 0)
                k = k - c1p * pltpu.roll(m, 32, 1) - c1m * pltpu.roll(m, LANES - 32, 1)
                k = k - c2p * turned2 - c2m * pltpu.roll(m, LANES - 4, 1)
                k = k - c3p * turned3 - c3m * pltpu.roll(m, LANES - 1, 1)
                comm.append(k)
                s = (
                    d1p * pltpu.roll(row1, 32, 1)
                    + d2p * pltpu.roll(tb.c2p * turned2, 4, 0)
                    + d3p * pltpu.roll(tb.c3p * turned3, 1, 0)
                )
                if t > 0:
                    s = s + (decay[0] * below[1] * root_left) * tile(z, below[0], c, t - 1)
                sand.append(s)
            phase = row_energy - column_energy[t]
            damping = (
                row_decay
                + (column_decay[t] + (dephasing[0] * i0f) * j0.astype(F32))
                + (dephasing[1] * i1f) * tb.j1
                + cross2 * tb.j2
                + cross3 * tb.j3
            )
            x, y = values
            lanes = slice(t * LANES, (t + 1) * LANES)
            out[here, 0, :, lanes] = tile(base, wide(here), 0, t) + scale * (
                damping * x - phase * y - comm[1] + sand[0]
            )
            out[here, 1, :, lanes] = tile(base, wide(here), 1, t) + scale * (
                damping * y + phase * x + comm[0] + sand[1]
            )
        return carry

    lax.fori_loop(0, UNITS, step, 0, unroll=4)
    wait_all(writes)


def start_all(copies):
    for copy in copies:
        copy.start()


def wait_all(copies):
    for copy in copies:
        copy.wait()


def put_slabs(place, tb, p, pair, both, s_i0, s_j1, s_j0, s_i2, s_c):
    lane, _ = iotas()
    half = (lax.broadcasted_iota(jnp.int32, (8, LANES), 0) >> 2) == 1 - place.gi2
    block = lane >> 5
    gj0 = place.gj0 == 1
    gi2 = place.gi2 == 1
    for par in range(2):
        i1 = 2 * pair + par
        n = p * 8 + i1
        for c in range(2):
            tiles = both[par][c]
            if p == 3:
                for t in range(TILES):
                    s_i0[i1, c, :, t * LANES : (t + 1) * LANES] = tiles[t]
                s_c[i1, c] = tiles[TILES - 1]
            s_j0[2 * n + c] = jnp.where(gj0, tiles[0], tiles[TILES - 1])
            packed = tiles[0]
            for t in range(1, TILES):
                turned = pltpu.roll(tiles[t], 32 * t, 1)
                packed = jnp.where(block == ((tb.edge1 + t) & 3), turned, packed)
            s_j1[2 * n + c] = packed
    for c in range(2):
        for t in range(TILES):
            even, odd = both[0][c][t], both[1][c][t]
            stays = jnp.where(gi2, even[0:8], odd[8:16])
            moves = pltpu.roll(jnp.where(gi2, odd[0:8], even[8:16]), 4, 0)
            entry = ((p * 4 + pair) * 2 + c) * 2 + t // 2
            s_i2[entry, (t % 2) * 8 : (t % 2) * 8 + 8] = jnp.where(half, stays, moves)


def slab_kernel(z, s_i0, s_j1, s_j0, s_i2, s_c):
    place = Place()
    tb = Tables(place)
    for p in range(4):

        def step(pair, carry, p=p):
            both = [
                [[tile(z, wide(unit_at(p, 2 * pair + par)), c, t) for t in range(TILES)] for c in range(2)]
                for par in range(2)
            ]
            put_slabs(place, tb, p, pair, both, s_i0, s_j1, s_j0, s_i2, s_c)
            return carry

        lax.fori_loop(0, 4, step, 0, unroll=True)


def i2_halo(place, h_i2, p, pair, par, c, t):
    small = h_i2[((p * 4 + pair) * 2 + c) * 2 + t // 2, (t % 2) * 8 : (t % 2) * 8 + 8]
    turned = pltpu.roll(small, 4, 0)
    return jnp.where(place.gi2 == par, turned, small)


def edge_kernel(scale, last, *refs):
    part, h_i0, h_j1, h_j0, h_i2, h_c = refs[:6]
    if last:
        amp, dec, roots, out_all, out_rest, block, sems = refs[6:]
        later = 16 * MOST
    else:
        amp, dec, roots, out, *slabs = refs[6:]
    place = Place()
    tb = Tables(place)
    up = place.upper == 1
    upf = place.upper.astype(F32)
    gj0f = place.gj0.astype(F32)
    gj1f = place.gj1.astype(F32)
    gi2f = place.gi2.astype(F32)
    copies = []
    decay = [scale * dec[0, q] for q in range(4)]
    u = [scale * amp[0, q] for q in range(4)]
    s1_base = (decay[1] * 2.0 * gj1f) * tb.at1
    s2_base = ((decay[2] * 2.0 * gi2f) * tb.at2 * tb.c2p)[0:8]
    k1_mask = (-2.0 * u[1]) * tb.at1
    k2_mask = (2.0 * u[2]) * tb.at2

    def one(p, pair, par, kept):
        i0 = jnp.where(up, 7 - p, p)
        below = jnp.where(up, p + 1, p - 1)
        below_in = (below >= 0) & (below <= 3)
        below = jnp.clip(below, 0, 3)
        root_below = jnp.where(below_in, roots[0, i0], 0.0)
        i1 = 2 * pair + par
        here = unit_at(p, i1)
        n = p * 8 + i1
        s1_less = roots[0, i1] * s1_base
        n_less = p * 8 + jnp.maximum(i1 - 1, 0)
        new = [[], []]
        for t in range(TILES):
            j0 = 4 * place.gj0 + t
            lanes = slice(t * LANES, (t + 1) * LANES)
            turn = (32 * (2 * tb.edge1 - 3 - t)) & (LANES - 1)
            comm = []
            sand = []
            for c in range(2):
                across = i2_halo(place, h_i2, p, pair, par, c, t)
                own = pltpu.roll(h_j1[2 * n + c], turn, 1)
                if par == 0:
                    lower = pltpu.roll(h_j1[2 * n_less + c], turn, 1)
                else:
                    lower = kept[c, t]
                kept[c, t] = own
                k = k2_mask * jnp.concatenate([across, across], axis=0) + k1_mask * own
                first = s2_base * pltpu.roll(across, 4, 1)
                s = s1_less * lower
                s = jnp.concatenate([s[0:8] + first, s[8:16]], axis=0)
                if p == 3:
                    k = k + (2.0 * u[0]) * h_i0[i1, c, :, lanes]
                    if t > 0:
                        s = s + (decay[0] * 2.0 * upf * roots[0, j0]) * h_i0[
                            i1, c, :, (t - 1) * LANES : t * LANES
                        ]
                    else:
                        s = s + (decay[0] * 4.0 * upf * gj0f) * h_c[i1, c]
                if t == 0 or t == TILES - 1:
                    on = gj0f if t == 0 else 1.0 - gj0f
                    k = k - (2.0 * u[0] * on) * h_j0[2 * n + c]
                if t == 0:
                    s = s + (decay[0] * 2.0 * gj0f * root_below) * h_j0[2 * (below * 8 + i1) + c]
                comm.append(k)
                sand.append(s)
            new[0].append(tile(part, here, 0, t) + (sand[0] - comm[1]))
            new[1].append(tile(part, here, 1, t) + (sand[1] + comm[0]))
        return here, new

    for p in range(4):

        def step(pair, carry, p=p):
            both = []
            kept = {}
            for par in range(2):
                here, new = one(p, pair, par, kept)
                for c in range(2):
                    for t in range(TILES):
                        out[here, c, :, t * LANES : (t + 1) * LANES] = new[c][t]
                both.append(new)
            put_slabs(place, tb, p, pair, both, *slabs)
            return carry

        def last_step(h, carry, p=p):
            kept = {}
            for a in range(4):
                here, new = one(p, 2 * h + a // 2, a % 2, kept)
                for c in range(2):
                    for t in range(TILES):
                        lanes = slice(t * LANES, (t + 1) * LANES)
                        at = (2 * a + c) * ROWS
                        block[here >> 2, at : at + ROWS, lanes] = new[c][t]
            return carry

        if last:
            lax.fori_loop(0, 2, last_step, 0, unroll=True)
            slots = pl.ds(2 * p, 2)
            rows = pl.ds(later, 128 - later)
            copies.append(pltpu.make_async_copy(block.at[slots], out_all.at[slots], sems.at[p]))
            copies.append(pltpu.make_async_copy(block.at[slots, rows], out_rest.at[slots], sems.at[4 + p]))
            start_all(copies[-2:])
        else:
            lax.fori_loop(0, 4, step, 0, unroll=True)
    wait_all(copies)


def gradient_kernel(z_in, rho_in, i0_in, j1_in, j0_in, i2_in, roots, grad, z, rho, h_i0, h_j1, h_j0, h_i2, sems):
    reads = []
    for source, target in (
        (z_in, z),
        (rho_in.at[:, pl.ds(4, 4)], rho),
        (i0_in, h_i0),
        (j1_in, h_j1),
        (j0_in, h_j0),
        (i2_in, h_i2),
    ):
        reads.append(pltpu.make_async_copy(source, target, sems.at[len(reads)]))
    start_all(reads)
    place = Place()
    tb = Tables(place)
    gj0f = place.gj0.astype(F32)
    wait_all(reads)
    k1_mask = -2.0 * tb.at1
    k2_mask = 2.0 * tb.at2

    def half_step(n, par, acc):
        p = n >> 2
        pair = n & 3
        i1 = 2 * pair + par
        unit = p * 8 + i1
        here = unit_at(p, i1)
        _, below, above, less, more = unit_neighbours(place, roots, p, i1)
        outer = jnp.where(p == 3, 2.0, 0.0)
        for t in range(TILES):
            j0 = 4 * place.gj0 + t
            turn = (32 * (2 * tb.edge1 - 3 - t)) & (LANES - 1)
            for c in range(2):
                m = tile(z, here, c, t)
                k0 = below[1] * tile(z, below[0], c, t) + above[1] * tile(z, above[0], c, t)
                k0 = k0 + outer * h_i0[i1, c, :, t * LANES : (t + 1) * LANES]
                if t > 0:
                    k0 = k0 - roots[0, j0] * tile(z, here, c, t - 1)
                if t < TILES - 1:
                    k0 = k0 - roots[0, j0 + 1] * tile(z, here, c, t + 1)
                if t == 0 or t == TILES - 1:
                    on = gj0f if t == 0 else 1.0 - gj0f
                    k0 = k0 - (2.0 * on) * h_j0[2 * unit + c]
                k1 = less[1] * tile(z, less[0], c, t) + more[1] * tile(z, more[0], c, t)
                k1 = k1 - tb.c1p * pltpu.roll(m, 32, 1) - tb.c1m * pltpu.roll(m, LANES - 32, 1)
                k1 = k1 + k1_mask * pltpu.roll(h_j1[2 * unit + c], turn, 1)
                k2 = tb.r2p * pltpu.roll(m, 4, 0) + tb.r2m * pltpu.roll(m, ROWS - 4, 0)
                k2 = k2 - tb.c2p * pltpu.roll(m, 4, 1) - tb.c2m * pltpu.roll(m, LANES - 4, 1)
                across = i2_halo(place, h_i2, p, pair, par, c, t)
                k2 = k2 + k2_mask * jnp.concatenate([across, across], axis=0)
                k3 = tb.r3p * pltpu.roll(m, 1, 0) + tb.r3m * pltpu.roll(m, ROWS - 1, 0)
                k3 = k3 - tb.c3p * pltpu.roll(m, 1, 1) - tb.c3m * pltpu.roll(m, LANES - 1, 1)
                other = rho[here >> 2, here & 3, 1 - c, :, t * LANES : (t + 1) * LANES]
                if c == 1:
                    other = -other
                acc = [acc[q] + k * other for q, k in enumerate((k0, k1, k2, k3))]
        return acc

    def step(n, carry):
        acc = list(carry)
        for par in range(2):
            acc = half_step(n, par, acc)
        return tuple(acc)

    start = tuple(jnp.zeros((ROWS, LANES), F32) for _ in range(4))
    total = lax.fori_loop(0, UNITS // 2, step, start, unroll=2)
    for q in range(4):
        grad[:, q * LANES : (q + 1) * LANES] = total[q][0:8] + total[q][8:16]


def chunk_lanes(g, t):
    start = (g // 2) * 1024 + t * 256 + (g % 2) * 128
    return slice(start, start + LANES)


def slice_rows(a):
    return pl.ds(32 * a, 32)


def pack_kernel(adjoint, state, out, plain, block, sems):
    upper = lax.axis_index("row") >> 3
    reads = []
    for m, x in enumerate((adjoint, state)):
        for a in range(4):
            rows = slice_rows(a)
            reads.append(pltpu.make_async_copy(x.at[:, rows], plain.at[m, :, rows], sems.at[4 * m + a]))
    writes = [pltpu.make_async_copy(block.at[:, at], out.at[:, at], sems.at[8 + at]) for at in range(8)]
    start_all(reads)
    for at in range(8):
        m, a = at // 4, at % 4
        reads[at].wait()
        for gi2 in range(2):
            for g in range(4):
                k = 4 * gi2 + jnp.where(upper == 1, 3 - g, g)
                for c in range(2):
                    for t in range(TILES):
                        block[k, at, c, :, t * LANES : (t + 1) * LANES] = plain[
                            m, c, 32 * a + 16 * gi2 : 32 * a + 16 * gi2 + 16, chunk_lanes(g, t)
                        ]
        writes[at].start()
    wait_all(writes)


def join_kernel(blocks, grad, out, sems):
    rows = 16 * (8 - MOST)
    copies = [pltpu.make_async_copy(blocks, out.at[:, pl.ds(0, rows)], sems.at[8])]
    for k in range(8):
        copies.append(pltpu.make_async_copy(grad, out.at[k, pl.ds(rows, 8)], sems.at[k]))
    start_all(copies)
    wait_all(copies)


def undeal(upper, index, source, first, out, base=None):
    a, c = index // 2, index % 2
    for gi2 in range(2):
        rows = slice(32 * a + 16 * gi2, 32 * a + 16 * gi2 + 16)
        for g in range(4):
            k = 4 * gi2 + jnp.where(upper == 1, 3 - g, g)
            for t in range(TILES):
                lanes = chunk_lanes(g, t)
                value = source[k, first : first + 16, t * LANES : (t + 1) * LANES]
                if base is not None:
                    value = base[c, rows, lanes] - value
                out[c, rows, lanes] = value


def start_kernel(blocks, start, held, plain, sems):
    upper = lax.axis_index("row") >> 3
    reads = [
        pltpu.make_async_copy(blocks.at[:, pl.ds(32 * a, 32)], held.at[:, pl.ds(32 * a, 32)], sems.at[a])
        for a in range(4)
    ]
    writes = [
        pltpu.make_async_copy(plain.at[:, slice_rows(a)], start.at[:, slice_rows(a)], sems.at[4 + a])
        for a in range(4)
    ]
    start_all(reads)
    for a in range(4):
        reads[a].wait()
        for c in range(2):
            undeal(upper, 2 * a + c, held, 32 * a + 16 * c, plain)
        writes[a].start()
    wait_all(writes)


def early_kernel(most, base, defect, held, held_base, plain, sems):
    upper = lax.axis_index("row") >> 3
    reads = []
    writes = []
    for a in range(EARLY):
        rows = pl.ds(32 * a, 32)
        reads.append(pltpu.make_async_copy(most.at[:, rows], held.at[:, rows], sems.at[3 * a]))
        reads.append(pltpu.make_async_copy(base.at[:, rows], held_base.at[:, rows], sems.at[3 * a + 1]))
        writes.append(pltpu.make_async_copy(plain.at[:, rows], defect.at[:, rows], sems.at[3 * a + 2]))
    start_all(reads)
    for a in range(EARLY):
        wait_all(reads[2 * a : 2 * a + 2])
        for c in range(2):
            index = 2 * a + c
            undeal(upper, index, held, 16 * index, plain, held_base)
        writes[a].start()
    wait_all(writes)


def late_kernel(partial, most, rest, base, defect, total, held_most, held_rest, held_base, plain, sems):
    del partial
    upper = lax.axis_index("row") >> 3
    rows = 16 * (8 - MOST)
    first = 32 * EARLY
    reads = [
        pltpu.make_async_copy(rest, held_rest, sems.at[0]),
        pltpu.make_async_copy(
            base.at[:, pl.ds(first, 128 - first)], held_base.at[:, pl.ds(first, 128 - first)], sems.at[1]
        ),
        pltpu.make_async_copy(
            most.at[:, pl.ds(first, 16 * MOST - first)], held_most.at[:, pl.ds(first, 16 * MOST - first)], sems.at[2]
        ),
    ]
    order = range(3, EARLY - 1, -1)
    writes = [
        pltpu.make_async_copy(plain.at[:, slice_rows(a)], defect.at[:, slice_rows(a)], sems.at[3 + a])
        for a in order
    ]
    start_all(reads)
    wait_all(reads)
    for at, a in enumerate(order):
        for c in range(2):
            index = 2 * a + c
            if index < MOST:
                undeal(upper, index, held_most, 16 * index, plain, held_base)
            else:
                undeal(upper, index, held_rest, 16 * (index - MOST), plain, held_base)
        writes[at].start()
    lane = lax.broadcasted_iota(jnp.int32, (1, 1, 4), 2)
    sums = jnp.zeros((1, 1, 4), F32)
    for q in range(4):
        part = held_rest[0, rows : rows + 8, q * LANES : (q + 1) * LANES]
        for k in range(1, 8):
            part = part + held_rest[k, rows : rows + 8, q * LANES : (q + 1) * LANES]
        sums = jnp.where(lane == q, jnp.sum(part) / ORDER, sums)
    total[...] = sums
    wait_all(writes)


def most_kernel(blocks, out):
    for k in range(8):
        out[k] = blocks[k, 0 : 16 * MOST]


VMEM = pl.BlockSpec(memory_space=pltpu.VMEM)
SMEM = pl.BlockSpec(memory_space=pltpu.SMEM)
ANY = pl.BlockSpec(memory_space=pl.ANY)
PARAMS = pltpu.CompilerParams(vmem_limit_bytes=16 * 1024 * 1024)
MOST = 5
EARLY = MOST // 2
UNIT_SHAPE = (UNITS, 2, ROWS, WIDTH)
PACKED_SHAPE = (8, 8, 2, ROWS, WIDTH)
PLAIN_SHAPE = (2, 128, ORDER)
BLOCKS_SHAPE = (8, 128, WIDTH)
MOST_SHAPE = (8, 16 * MOST, WIDTH)
REST_SHAPE = (8, 16 * (8 - MOST), WIDTH)
JOINED_SHAPE = (8, 16 * (8 - MOST) + 8, WIDTH)


SLAB_SHAPES = [(8, 2, ROWS, WIDTH)] + [(64, ROWS, LANES)] * 3 + [(8, 2, ROWS, LANES)]


def shape(dims):
    return jax.ShapeDtypeStruct(dims, F32)


def copies(count):
    return pltpu.SemaphoreType.DMA((count,))


def room(dims):
    return pltpu.VMEM(dims, F32)


def call(kernel, outs, args, scalars=(), flops=0, size=4 << 20, scratch=(), name=None, specs=None, out_specs=None, **more):
    out_shape = [shape(s) if isinstance(s, tuple) else s for s in outs]
    return pl.pallas_call(
        kernel,
        out_shape=out_shape,
        in_specs=(specs or [VMEM] * len(args)) + [SMEM] * len(scalars),
        out_specs=out_specs or [VMEM] * len(outs),
        scratch_shapes=list(scratch),
        compiler_params=PARAMS,
        cost_estimate=pl.CostEstimate(flops=flops, bytes_accessed=size, transcendentals=0),
        name=name,
        **more,
    )(*args, *scalars)


def in_hbm(x):
    return pltpu.with_memory_space_constraint(x, pltpu.HBM)


def hbm(dims):
    return pltpu.HBM(dims, F32)


def pack(adjoint, state):
    (packed,) = call(
        pack_kernel,
        [hbm(PACKED_SHAPE)],
        [in_hbm(adjoint), in_hbm(state)],
        specs=[ANY, ANY],
        out_specs=[ANY],
        scratch=[room((2, *PLAIN_SHAPE)), room(PACKED_SHAPE), copies(16)],
        name="pack_blocks",
    )
    return packed


def regroup(x):
    return lax.all_to_all(x, "row", 0, 0, axis_index_groups=GROUPS, tiled=True)


def earlier(x):
    return lax.ppermute(x, "seg", [(i + 1, i) for i in range(7)])


def exchange(slabs, perms):
    return [lax.ppermute(s, "row", perm) for s, perm in zip(slabs, perms)]


def body(
    terminal_adjoint,
    midpoint_state,
    controls,
    detuning,
    anharmonicity,
    decay_rate,
    dephasing,
    cross_kerr,
):
    amp = controls[0]
    dec = decay_rate[None]
    roots = jnp.asarray(ROOTS)[None]
    full = (amp, detuning[None], anharmonicity[None], dec, dephasing[None], cross_kerr[None], roots)
    few = (amp, dec, roots)
    terminal = terminal_adjoint[0]
    both = regroup(pack(terminal, midpoint_state[0, 0]))
    base = both.reshape(2 * UNITS, 2, ROWS, WIDTH)
    slabs = call(slab_kernel, SLAB_SHAPES, [base], name="slabs")
    current = base
    for n in range(3):
        scale = STEP if n == 2 else 0.5 * STEP
        halos = exchange(slabs, (PERM_I0, PERM_J1, PERM_J0, PERM_I2, PERM_CORNER))
        part, *middle = call(
            lambda *refs, n=n, scale=scale: local_kernel(scale, n, *refs),
            [UNIT_SHAPE] + [hbm(UNIT_SHAPE)] * (n == 2),
            [current, base],
            full,
            flops=30 << 20,
            size=6 << 20,
            out_specs=[VMEM] + [ANY] * (n == 2),
            scratch=[copies(1)] if n == 2 else [],
            name="local_terms",
        )
        if n < 2:
            current, *slabs = call(
                lambda *refs, scale=scale: edge_kernel(scale, False, *refs),
                [UNIT_SHAPE, *SLAB_SHAPES],
                [part, *halos],
                few,
                flops=5 << 20,
                size=8 << 20,
                name="edge_terms",
            )
    final, rest = call(
        lambda *refs: edge_kernel(STEP, True, *refs),
        [hbm(BLOCKS_SHAPE), hbm(REST_SHAPE)],
        [part, *halos],
        few,
        flops=5 << 20,
        size=6 << 20,
        out_specs=[ANY, ANY],
        scratch=[room(BLOCKS_SHAPE), copies(8)],
        name="edge_terms",
    )
    here = regroup(final)
    rest_next = earlier(rest)
    (grad,) = call(
        gradient_kernel,
        [(8, WIDTH)],
        [in_hbm(x) for x in (*middle, both, *halos[:4])],
        (roots,),
        flops=30 << 20,
        size=6 << 20,
        specs=[ANY] * 6,
        scratch=[room(UNIT_SHAPE), room((8, 4, 2, ROWS, WIDTH)), *map(room, SLAB_SHAPES[:4]), copies(6)],
        name="gradient",
    )
    grad = grad + lax.ppermute(grad, "row", PERM_I0)
    (joined,) = call(
        join_kernel,
        [hbm(JOINED_SHAPE)],
        [rest_next, grad],
        out_specs=[ANY],
        scratch=[copies(9)],
        name="join_blocks",
    )
    here, joined = lax.optimization_barrier((here, joined))
    rest_here = regroup(joined)
    (most,) = call(most_kernel, [MOST_SHAPE], [here], name="most_blocks")
    most_next = earlier(most)
    (start,) = call(
        start_kernel,
        [hbm(PLAIN_SHAPE)],
        [here],
        specs=[ANY],
        out_specs=[ANY],
        scratch=[room(BLOCKS_SHAPE), room(PLAIN_SHAPE), copies(8)],
        name="start_rows",
    )
    terminal = in_hbm(terminal)
    (defect,) = call(
        early_kernel,
        [hbm(PLAIN_SHAPE)],
        [most_next, terminal],
        specs=[ANY, ANY],
        out_specs=[ANY],
        scratch=[room(MOST_SHAPE), room(PLAIN_SHAPE), room(PLAIN_SHAPE), copies(3 * EARLY)],
        name="defect_early",
    )
    start, defect, rest_here = lax.optimization_barrier((start, defect, rest_here))
    defect, totals = call(
        late_kernel,
        [hbm(PLAIN_SHAPE), (1, 1, 4)],
        [defect, most_next, rest_here, terminal],
        specs=[ANY] * 4,
        out_specs=[ANY, VMEM],
        scratch=[room(MOST_SHAPE), room(JOINED_SHAPE), room(PLAIN_SHAPE), room(PLAIN_SHAPE), copies(7)],
        name="defect_late",
        input_output_aliases={0: 0},
    )
    return start[None], defect[None], totals


def solution(mesh):
    return jax.shard_map(
        body,
        mesh=mesh,
        in_specs=(
            P("seg", None, "row", None),
            P("seg", None, None, "row", None),
            P("seg", None, None),
            P(),
            P(),
            P(),
            P(),
            P(),
        ),
        out_specs=(P("seg", None, "row", None), P("seg", None, "row", None), P("seg", None, None)),
        check_vma=False,
    )
```

```python
import jax
import jax.numpy as jnp
import numpy as np
from jax import lax
from jax.experimental import pallas as pl
from jax.experimental.pallas import tpu as pltpu
from jax.sharding import PartitionSpec as P


ORDER = 2048
STEP = 0.01
UNITS = 32
ROWS = 16
LANES = 128
TILES = 4
WIDTH = TILES * LANES
F32 = jnp.float32

GROUPS = [
    [4 * y + z for y in (0, 1) for z in (0, 1, 3, 2)],
    [4 * y + z for y in (3, 2) for z in (2, 3, 1, 0)],
]
Y_OUTER = {0: 3, 3: 0, 1: 2, 2: 1}
Y_INNER = {0: 1, 1: 0, 2: 3, 3: 2}


def pairs_y(flip):
    return [(4 * y + z, 4 * flip[y] + z) for y in range(4) for z in range(4)]


def pairs_z(flip):
    return [(4 * y + z, 4 * y + flip[z]) for y in range(4) for z in range(4)]


PERM_I0 = pairs_y(Y_OUTER)
PERM_I2 = pairs_y(Y_INNER)
PERM_J0 = pairs_z(Y_OUTER)
PERM_J1 = pairs_z(Y_INNER)
PERM_CORNER = [(4 * y + z, 4 * Y_OUTER[y] + Y_OUTER[z]) for y in (0, 1) for z in (0, 1)]
ROOTS = np.sqrt(np.arange(16)).astype(np.float32)


class Place:
    def __init__(self):
        row = lax.axis_index("row")
        y = row >> 2
        z = row & 3
        self.upper = y >> 1
        self.gi2 = jnp.where((y == 1) | (y == 2), 1, 0)
        self.gj0 = z >> 1
        self.gj1 = jnp.where((z == 1) | (z == 2), 1, 0)


def unit_at(p, i1):
    odd = p & 1
    return ((p >> 1) << 4) + (((i1 >> 2) ^ (3 * odd)) << 2) + (i1 & 3)


def wide(unit):
    return unit + ((unit >> 2) << 2)


def iotas():
    lane = lax.broadcasted_iota(jnp.int32, (ROWS, LANES), 1)
    sub = lax.broadcasted_iota(jnp.int32, (ROWS, LANES), 0)
    return lane, sub


class Tables:
    def __init__(self, place):
        lane, sub = iotas()
        low1 = lane >> 5
        self.j1 = (low1 + 4 * place.gj1).astype(F32)
        self.j2 = ((lane >> 2) & 7).astype(F32)
        self.j3 = (lane & 3).astype(F32)
        low2 = sub >> 2
        self.i2 = (low2 + 4 * place.gi2).astype(F32)
        self.i3 = (sub & 3).astype(F32)
        self.c1p = jnp.where(low1 > 0, jnp.sqrt(self.j1), 0.0)
        self.c1m = jnp.where(low1 < 3, jnp.sqrt(self.j1 + 1.0), 0.0)
        self.c2p = jnp.sqrt(self.j2)
        self.c2m = jnp.where(self.j2 < 7.0, jnp.sqrt(self.j2 + 1.0), 0.0)
        self.c3p = jnp.sqrt(self.j3)
        self.c3m = jnp.where(self.j3 < 3.0, jnp.sqrt(self.j3 + 1.0), 0.0)
        self.r2p = jnp.where(low2 > 0, jnp.sqrt(self.i2), 0.0)
        self.r2m = jnp.where(low2 < 3, jnp.sqrt(self.i2 + 1.0), 0.0)
        self.r3p = jnp.sqrt(self.i3)
        self.r3m = jnp.where(self.i3 < 3.0, jnp.sqrt(self.i3 + 1.0), 0.0)
        edge1 = jnp.where(place.gj1 == 1, 0, 3)
        edge2 = jnp.where(place.gi2 == 1, 0, 3)
        self.edge1 = edge1
        self.at1 = (low1 == edge1).astype(F32)
        self.at2 = (low2 == edge2).astype(F32)


def drift(levels, detuning, anharmonicity, cross_kerr):
    total = 0.0
    for q in range(4):
        n = levels[q]
        total = total + detuning[q] * n - 0.5 * anharmonicity[q] * n * (n - 1.0)
    k = 0
    for a in range(4):
        for b in range(a + 1, 4):
            total = total - cross_kerr[k] * levels[a] * levels[b]
            k += 1
    return total


def decay_part(levels, decay, dephasing):
    total = 0.0
    for q in range(4):
        n = levels[q]
        total = total - 0.5 * decay[q] * n - 0.5 * dephasing[q] * n * n
    return total


def tile(ref, unit, c, t):
    return ref[unit, c, :, t * LANES : (t + 1) * LANES]


def level_of(place, p):
    return jnp.where(place.upper == 1, 7 - p, p)


def unit_neighbours(place, roots, p, i1, at=unit_at):
    up = place.upper == 1
    i0 = level_of(place, p)
    below = jnp.where(up, p + 1, p - 1)
    above = jnp.where(up, p - 1, p + 1)
    root_below = jnp.where((below >= 0) & (below <= 3), roots[0, i0], 0.0)
    root_above = jnp.where((above >= 0) & (above <= 3), roots[0, i0 + 1], 0.0)
    return (
        i0,
        (at(jnp.clip(below, 0, 3), i1), root_below),
        (at(jnp.clip(above, 0, 3), i1), root_above),
        (at(p, jnp.maximum(i1 - 1, 0)), roots[0, i1]),
        (at(p, jnp.minimum(i1 + 1, 7)), jnp.where(i1 < 7, roots[0, i1 + 1], 0.0)),
    )


def local_kernel(scale, n, *refs):
    z, base, *scalars, out = refs[:10]
    writes = []
    if n == 2:
        z_out, sems = refs[10:]
        writes = [pltpu.make_async_copy(z, z_out, sems.at[0])]
    start_all(writes)
    amp, det, anh, dec, dep, kerr, roots = scalars
    def at(p, i1):
        return unit_at(p, i1) if n else wide(unit_at(p, i1))

    place = Place()
    tb = Tables(place)
    detuning = [det[0, q] for q in range(4)]
    anharm = [anh[0, q] for q in range(4)]
    decay = [dec[0, q] for q in range(4)]
    dephasing = [dep[0, q] for q in range(4)]
    cross = [kerr[0, k] for k in range(6)]
    u = [amp[0, q] for q in range(4)]
    column_energy = []
    column_decay = []
    for t in range(TILES):
        j0 = (4 * place.gj0 + t).astype(F32)
        levels = [j0, tb.j1, tb.j2, tb.j3]
        column_energy.append(drift(levels, detuning, anharm, cross))
        column_decay.append(decay_part(levels, decay, dephasing))
    cross2 = dephasing[2] * tb.i2
    cross3 = dephasing[3] * tb.i3
    c1m, c2m, c3m = u[1] * tb.c1m, u[2] * tb.c2m, u[3] * tb.c3m
    c1p, c2p, c3p = u[1] * tb.c1p, u[2] * tb.c2p, u[3] * tb.c3p
    r2m, r3m = u[2] * tb.r2m, u[3] * tb.r3m
    r2p, r3p = u[2] * tb.r2p, u[3] * tb.r3p
    d2p, d3p = decay[2] * tb.r2p, decay[3] * tb.r3p

    def step(unit, carry):
        p = unit >> 3
        i1 = unit & 7
        here = unit_at(p, i1)
        mine = at(p, i1)
        i0, below, above, less, more = unit_neighbours(place, roots, p, i1, at)
        i0f = i0.astype(F32)
        i1f = i1.astype(F32)
        rows = [i0f, i1f, tb.i2, tb.i3]
        row_energy = drift(rows, detuning, anharm, cross)
        row_decay = decay_part(rows, decay, dephasing)
        d1p = (decay[1] * less[1]) * tb.c1p
        for t in range(TILES):
            j0 = 4 * place.gj0 + t
            root_left = roots[0, j0]
            root_right = roots[0, j0 + 1]
            comm = []
            sand = []
            values = []
            for c in range(2):
                m = tile(z, mine, c, t)
                values.append(m)
                turned2 = pltpu.roll(m, 4, 1)
                turned3 = pltpu.roll(m, 1, 1)
                row1 = tile(z, less[0], c, t)
                row0 = tile(z, below[0], c, t)
                k = (u[0] * below[1]) * row0 + (u[0] * above[1]) * tile(z, above[0], c, t)
                k = k + (u[1] * less[1]) * row1 + (u[1] * more[1]) * tile(z, more[0], c, t)
                if t > 0:
                    k = k - (u[0] * root_left) * tile(z, mine, c, t - 1)
                if t < TILES - 1:
                    k = k - (u[0] * root_right) * tile(z, mine, c, t + 1)
                k = k + r2p * pltpu.roll(m, 4, 0) + r2m * pltpu.roll(m, ROWS - 4, 0)
                k = k + r3p * pltpu.roll(m, 1, 0) + r3m * pltpu.roll(m, ROWS - 1, 0)
                k = k - c1p * pltpu.roll(m, 32, 1) - c1m * pltpu.roll(m, LANES - 32, 1)
                k = k - c2p * turned2 - c2m * pltpu.roll(m, LANES - 4, 1)
                k = k - c3p * turned3 - c3m * pltpu.roll(m, LANES - 1, 1)
                comm.append(k)
                s = (
                    d1p * pltpu.roll(row1, 32, 1)
                    + d2p * pltpu.roll(tb.c2p * turned2, 4, 0)
                    + d3p * pltpu.roll(tb.c3p * turned3, 1, 0)
                )
                if t > 0:
                    s = s + (decay[0] * below[1] * root_left) * tile(z, below[0], c, t - 1)
                sand.append(s)
            phase = row_energy - column_energy[t]
            damping = (
                row_decay
                + (column_decay[t] + (dephasing[0] * i0f) * j0.astype(F32))
                + (dephasing[1] * i1f) * tb.j1
                + cross2 * tb.j2
                + cross3 * tb.j3
            )
            x, y = values
            lanes = slice(t * LANES, (t + 1) * LANES)
            out[here, 0, :, lanes] = tile(base, wide(here), 0, t) + scale * (
                damping * x - phase * y - comm[1] + sand[0]
            )
            out[here, 1, :, lanes] = tile(base, wide(here), 1, t) + scale * (
                damping * y + phase * x + comm[0] + sand[1]
            )
        return carry

    lax.fori_loop(0, UNITS, step, 0, unroll=4)
    wait_all(writes)


def start_all(copies):
    for copy in copies:
        copy.start()


def wait_all(copies):
    for copy in copies:
        copy.wait()


def put_slabs(place, tb, p, pair, both, s_i0, s_j1, s_j0, s_i2, s_c):
    lane, _ = iotas()
    half = (lax.broadcasted_iota(jnp.int32, (8, LANES), 0) >> 2) == 1 - place.gi2
    block = lane >> 5
    gj0 = place.gj0 == 1
    gi2 = place.gi2 == 1
    for par in range(2):
        i1 = 2 * pair + par
        n = p * 8 + i1
        for c in range(2):
            tiles = both[par][c]
            if p == 3:
                for t in range(TILES):
                    s_i0[i1, c, :, t * LANES : (t + 1) * LANES] = tiles[t]
                s_c[i1, c] = tiles[TILES - 1]
            s_j0[2 * n + c] = jnp.where(gj0, tiles[0], tiles[TILES - 1])
            packed = tiles[0]
            for t in range(1, TILES):
                turned = pltpu.roll(tiles[t], 32 * t, 1)
                packed = jnp.where(block == ((tb.edge1 + t) & 3), turned, packed)
            s_j1[2 * n + c] = packed
    for c in range(2):
        for t in range(TILES):
            even, odd = both[0][c][t], both[1][c][t]
            stays = jnp.where(gi2, even[0:8], odd[8:16])
            moves = pltpu.roll(jnp.where(gi2, odd[0:8], even[8:16]), 4, 0)
            entry = ((p * 4 + pair) * 2 + c) * 2 + t // 2
            s_i2[entry, (t % 2) * 8 : (t % 2) * 8 + 8] = jnp.where(half, stays, moves)


def slab_kernel(z, s_i0, s_j1, s_j0, s_i2, s_c):
    place = Place()
    tb = Tables(place)
    for p in range(4):

        def step(pair, carry, p=p):
            both = [
                [[tile(z, wide(unit_at(p, 2 * pair + par)), c, t) for t in range(TILES)] for c in range(2)]
                for par in range(2)
            ]
            put_slabs(place, tb, p, pair, both, s_i0, s_j1, s_j0, s_i2, s_c)
            return carry

        lax.fori_loop(0, 4, step, 0, unroll=True)


def i2_halo(place, h_i2, p, pair, par, c, t):
    small = h_i2[((p * 4 + pair) * 2 + c) * 2 + t // 2, (t % 2) * 8 : (t % 2) * 8 + 8]
    turned = pltpu.roll(small, 4, 0)
    return jnp.where(place.gi2 == par, turned, small)


def edge_kernel(scale, last, *refs):
    part, h_i0, h_j1, h_j0, h_i2, h_c = refs[:6]
    if last:
        amp, dec, roots, out_all, out_rest, block, sems = refs[6:]
        later = 16 * MOST
    else:
        amp, dec, roots, out, *slabs = refs[6:]
    place = Place()
    tb = Tables(place)
    up = place.upper == 1
    upf = place.upper.astype(F32)
    gj0f = place.gj0.astype(F32)
    gj1f = place.gj1.astype(F32)
    gi2f = place.gi2.astype(F32)
    copies = []
    decay = [scale * dec[0, q] for q in range(4)]
    u = [scale * amp[0, q] for q in range(4)]
    s1_base = (decay[1] * 2.0 * gj1f) * tb.at1
    s2_base = ((decay[2] * 2.0 * gi2f) * tb.at2 * tb.c2p)[0:8]
    k1_mask = (-2.0 * u[1]) * tb.at1
    k2_mask = (2.0 * u[2]) * tb.at2

    def one(p, pair, par, kept):
        i0 = jnp.where(up, 7 - p, p)
        below = jnp.where(up, p + 1, p - 1)
        below_in = (below >= 0) & (below <= 3)
        below = jnp.clip(below, 0, 3)
        root_below = jnp.where(below_in, roots[0, i0], 0.0)
        i1 = 2 * pair + par
        here = unit_at(p, i1)
        n = p * 8 + i1
        s1_less = roots[0, i1] * s1_base
        n_less = p * 8 + jnp.maximum(i1 - 1, 0)
        new = [[], []]
        for t in range(TILES):
            j0 = 4 * place.gj0 + t
            lanes = slice(t * LANES, (t + 1) * LANES)
            turn = (32 * (2 * tb.edge1 - 3 - t)) & (LANES - 1)
            comm = []
            sand = []
            for c in range(2):
                across = i2_halo(place, h_i2, p, pair, par, c, t)
                own = pltpu.roll(h_j1[2 * n + c], turn, 1)
                if par == 0:
                    lower = pltpu.roll(h_j1[2 * n_less + c], turn, 1)
                else:
                    lower = kept[c, t]
                kept[c, t] = own
                k = k2_mask * jnp.concatenate([across, across], axis=0) + k1_mask * own
                first = s2_base * pltpu.roll(across, 4, 1)
                s = s1_less * lower
                s = jnp.concatenate([s[0:8] + first, s[8:16]], axis=0)
                if p == 3:
                    k = k + (2.0 * u[0]) * h_i0[i1, c, :, lanes]
                    if t > 0:
                        s = s + (decay[0] * 2.0 * upf * roots[0, j0]) * h_i0[
                            i1, c, :, (t - 1) * LANES : t * LANES
                        ]
                    else:
                        s = s + (decay[0] * 4.0 * upf * gj0f) * h_c[i1, c]
                if t == 0 or t == TILES - 1:
                    on = gj0f if t == 0 else 1.0 - gj0f
                    k = k - (2.0 * u[0] * on) * h_j0[2 * n + c]
                if t == 0:
                    s = s + (decay[0] * 2.0 * gj0f * root_below) * h_j0[2 * (below * 8 + i1) + c]
                comm.append(k)
                sand.append(s)
            new[0].append(tile(part, here, 0, t) + (sand[0] - comm[1]))
            new[1].append(tile(part, here, 1, t) + (sand[1] + comm[0]))
        return here, new

    for p in range(4):

        def step(pair, carry, p=p):
            both = []
            kept = {}
            for par in range(2):
                here, new = one(p, pair, par, kept)
                for c in range(2):
                    for t in range(TILES):
                        out[here, c, :, t * LANES : (t + 1) * LANES] = new[c][t]
                both.append(new)
            put_slabs(place, tb, p, pair, both, *slabs)
            return carry

        def last_step(h, carry, p=p):
            kept = {}
            for a in range(4):
                here, new = one(p, 2 * h + a // 2, a % 2, kept)
                for c in range(2):
                    for t in range(TILES):
                        lanes = slice(t * LANES, (t + 1) * LANES)
                        at = (2 * a + c) * ROWS
                        block[here >> 2, at : at + ROWS, lanes] = new[c][t]
            return carry

        if last:
            lax.fori_loop(0, 2, last_step, 0, unroll=True)
            slots = pl.ds(2 * p, 2)
            rows = pl.ds(later, 128 - later)
            copies.append(pltpu.make_async_copy(block.at[slots], out_all.at[slots], sems.at[p]))
            copies.append(pltpu.make_async_copy(block.at[slots, rows], out_rest.at[slots], sems.at[4 + p]))
            start_all(copies[-2:])
        else:
            lax.fori_loop(0, 4, step, 0, unroll=True)
    wait_all(copies)


def gradient_kernel(z_in, rho_in, i0_in, j1_in, j0_in, i2_in, roots, grad, z, rho, h_i0, h_j1, h_j0, h_i2, sems):
    reads = []
    for source, target in (
        (z_in, z),
        (rho_in.at[:, pl.ds(4, 4)], rho),
        (i0_in, h_i0),
        (j1_in, h_j1),
        (j0_in, h_j0),
        (i2_in, h_i2),
    ):
        reads.append(pltpu.make_async_copy(source, target, sems.at[len(reads)]))
    start_all(reads)
    place = Place()
    tb = Tables(place)
    gj0f = place.gj0.astype(F32)
    wait_all(reads)
    k1_mask = -2.0 * tb.at1
    k2_mask = 2.0 * tb.at2

    def half_step(n, par, acc):
        p = n >> 2
        pair = n & 3
        i1 = 2 * pair + par
        unit = p * 8 + i1
        here = unit_at(p, i1)
        _, below, above, less, more = unit_neighbours(place, roots, p, i1)
        outer = jnp.where(p == 3, 2.0, 0.0)
        for t in range(TILES):
            j0 = 4 * place.gj0 + t
            turn = (32 * (2 * tb.edge1 - 3 - t)) & (LANES - 1)
            for c in range(2):
                m = tile(z, here, c, t)
                k0 = below[1] * tile(z, below[0], c, t) + above[1] * tile(z, above[0], c, t)
                k0 = k0 + outer * h_i0[i1, c, :, t * LANES : (t + 1) * LANES]
                if t > 0:
                    k0 = k0 - roots[0, j0] * tile(z, here, c, t - 1)
                if t < TILES - 1:
                    k0 = k0 - roots[0, j0 + 1] * tile(z, here, c, t + 1)
                if t == 0 or t == TILES - 1:
                    on = gj0f if t == 0 else 1.0 - gj0f
                    k0 = k0 - (2.0 * on) * h_j0[2 * unit + c]
                k1 = less[1] * tile(z, less[0], c, t) + more[1] * tile(z, more[0], c, t)
                k1 = k1 - tb.c1p * pltpu.roll(m, 32, 1) - tb.c1m * pltpu.roll(m, LANES - 32, 1)
                k1 = k1 + k1_mask * pltpu.roll(h_j1[2 * unit + c], turn, 1)
                k2 = tb.r2p * pltpu.roll(m, 4, 0) + tb.r2m * pltpu.roll(m, ROWS - 4, 0)
                k2 = k2 - tb.c2p * pltpu.roll(m, 4, 1) - tb.c2m * pltpu.roll(m, LANES - 4, 1)
                across = i2_halo(place, h_i2, p, pair, par, c, t)
                k2 = k2 + k2_mask * jnp.concatenate([across, across], axis=0)
                k3 = tb.r3p * pltpu.roll(m, 1, 0) + tb.r3m * pltpu.roll(m, ROWS - 1, 0)
                k3 = k3 - tb.c3p * pltpu.roll(m, 1, 1) - tb.c3m * pltpu.roll(m, LANES - 1, 1)
                other = rho[here >> 2, here & 3, 1 - c, :, t * LANES : (t + 1) * LANES]
                if c == 1:
                    other = -other
                acc = [acc[q] + k * other for q, k in enumerate((k0, k1, k2, k3))]
        return acc

    def step(n, carry):
        acc = list(carry)
        for par in range(2):
            acc = half_step(n, par, acc)
        return tuple(acc)

    start = tuple(jnp.zeros((ROWS, LANES), F32) for _ in range(4))
    total = lax.fori_loop(0, UNITS // 2, step, start, unroll=2)
    for q in range(4):
        grad[:, q * LANES : (q + 1) * LANES] = total[q][0:8] + total[q][8:16]


def chunk_lanes(g, t):
    start = (g // 2) * 1024 + t * 256 + (g % 2) * 128
    return slice(start, start + LANES)


def slice_rows(a):
    return pl.ds(32 * a, 32)


def pack_kernel(adjoint, state, out, plain, block, sems):
    upper = lax.axis_index("row") >> 3
    reads = []
    for m, x in enumerate((adjoint, state)):
        for a in range(4):
            rows = slice_rows(a)
            reads.append(pltpu.make_async_copy(x.at[:, rows], plain.at[m, :, rows], sems.at[4 * m + a]))
    writes = [pltpu.make_async_copy(block.at[:, at], out.at[:, at], sems.at[8 + at]) for at in range(8)]
    start_all(reads)
    for at in range(8):
        m, a = at // 4, at % 4
        reads[at].wait()
        for gi2 in range(2):
            for g in range(4):
                k = 4 * gi2 + jnp.where(upper == 1, 3 - g, g)
                for c in range(2):
                    for t in range(TILES):
                        block[k, at, c, :, t * LANES : (t + 1) * LANES] = plain[
                            m, c, 32 * a + 16 * gi2 : 32 * a + 16 * gi2 + 16, chunk_lanes(g, t)
                        ]
        writes[at].start()
    wait_all(writes)


def join_kernel(blocks, grad, out, sems):
    rows = 16 * (8 - MOST)
    copies = [pltpu.make_async_copy(blocks, out.at[:, pl.ds(0, rows)], sems.at[8])]
    for k in range(8):
        copies.append(pltpu.make_async_copy(grad, out.at[k, pl.ds(rows, 8)], sems.at[k]))
    start_all(copies)
    wait_all(copies)


def undeal(upper, index, source, first, out, base=None):
    a, c = index // 2, index % 2
    for gi2 in range(2):
        rows = slice(32 * a + 16 * gi2, 32 * a + 16 * gi2 + 16)
        for g in range(4):
            k = 4 * gi2 + jnp.where(upper == 1, 3 - g, g)
            for t in range(TILES):
                lanes = chunk_lanes(g, t)
                value = source[k, first : first + 16, t * LANES : (t + 1) * LANES]
                if base is not None:
                    value = base[c, rows, lanes] - value
                out[c, rows, lanes] = value


def start_kernel(blocks, start, held, plain, sems):
    upper = lax.axis_index("row") >> 3
    reads = [
        pltpu.make_async_copy(blocks.at[:, pl.ds(32 * a, 32)], held.at[:, pl.ds(32 * a, 32)], sems.at[a])
        for a in range(4)
    ]
    writes = [
        pltpu.make_async_copy(plain.at[:, slice_rows(a)], start.at[:, slice_rows(a)], sems.at[4 + a])
        for a in range(4)
    ]
    start_all(reads)
    for a in range(4):
        reads[a].wait()
        for c in range(2):
            undeal(upper, 2 * a + c, held, 32 * a + 16 * c, plain)
        writes[a].start()
    wait_all(writes)


def early_kernel(most, base, defect, held, held_base, plain, sems):
    upper = lax.axis_index("row") >> 3
    reads = []
    writes = []
    for a in range(EARLY):
        rows = pl.ds(32 * a, 32)
        reads.append(pltpu.make_async_copy(most.at[:, rows], held.at[:, rows], sems.at[3 * a]))
        reads.append(pltpu.make_async_copy(base.at[:, rows], held_base.at[:, rows], sems.at[3 * a + 1]))
        writes.append(pltpu.make_async_copy(plain.at[:, rows], defect.at[:, rows], sems.at[3 * a + 2]))
    start_all(reads)
    for a in range(EARLY):
        wait_all(reads[2 * a : 2 * a + 2])
        for c in range(2):
            index = 2 * a + c
            undeal(upper, index, held, 16 * index, plain, held_base)
        writes[a].start()
    wait_all(writes)


def late_kernel(partial, most, rest, base, defect, total, held_most, held_rest, held_base, plain, sems):
    del partial
    upper = lax.axis_index("row") >> 3
    rows = 16 * (8 - MOST)
    first = 32 * EARLY
    reads = [
        pltpu.make_async_copy(rest, held_rest, sems.at[0]),
        pltpu.make_async_copy(
            base.at[:, pl.ds(first, 128 - first)], held_base.at[:, pl.ds(first, 128 - first)], sems.at[1]
        ),
        pltpu.make_async_copy(
            most.at[:, pl.ds(first, 16 * MOST - first)], held_most.at[:, pl.ds(first, 16 * MOST - first)], sems.at[2]
        ),
    ]
    order = range(3, EARLY - 1, -1)
    writes = [
        pltpu.make_async_copy(plain.at[:, slice_rows(a)], defect.at[:, slice_rows(a)], sems.at[3 + a])
        for a in order
    ]
    start_all(reads)
    wait_all(reads)
    for at, a in enumerate(order):
        for c in range(2):
            index = 2 * a + c
            if index < MOST:
                undeal(upper, index, held_most, 16 * index, plain, held_base)
            else:
                undeal(upper, index, held_rest, 16 * (index - MOST), plain, held_base)
        writes[at].start()
    lane = lax.broadcasted_iota(jnp.int32, (1, 1, 4), 2)
    sums = jnp.zeros((1, 1, 4), F32)
    for q in range(4):
        part = held_rest[0, rows : rows + 8, q * LANES : (q + 1) * LANES]
        for k in range(1, 8):
            part = part + held_rest[k, rows : rows + 8, q * LANES : (q + 1) * LANES]
        sums = jnp.where(lane == q, jnp.sum(part) / ORDER, sums)
    total[...] = sums
    wait_all(writes)


def most_kernel(blocks, out):
    for k in range(8):
        out[k] = blocks[k, 0 : 16 * MOST]


VMEM = pl.BlockSpec(memory_space=pltpu.VMEM)
SMEM = pl.BlockSpec(memory_space=pltpu.SMEM)
ANY = pl.BlockSpec(memory_space=pl.ANY)
PARAMS = pltpu.CompilerParams(vmem_limit_bytes=16 * 1024 * 1024)
MOST = 5
EARLY = MOST // 2
UNIT_SHAPE = (UNITS, 2, ROWS, WIDTH)
PACKED_SHAPE = (8, 8, 2, ROWS, WIDTH)
PLAIN_SHAPE = (2, 128, ORDER)
BLOCKS_SHAPE = (8, 128, WIDTH)
MOST_SHAPE = (8, 16 * MOST, WIDTH)
REST_SHAPE = (8, 16 * (8 - MOST), WIDTH)
JOINED_SHAPE = (8, 16 * (8 - MOST) + 8, WIDTH)


SLAB_SHAPES = [(8, 2, ROWS, WIDTH)] + [(64, ROWS, LANES)] * 3 + [(8, 2, ROWS, LANES)]


def shape(dims):
    return jax.ShapeDtypeStruct(dims, F32)


def copies(count):
    return pltpu.SemaphoreType.DMA((count,))


def room(dims):
    return pltpu.VMEM(dims, F32)


def call(kernel, outs, args, scalars=(), flops=0, size=4 << 20, scratch=(), name=None, specs=None, out_specs=None, **more):
    out_shape = [shape(s) if isinstance(s, tuple) else s for s in outs]
    return pl.pallas_call(
        kernel,
        out_shape=out_shape,
        in_specs=(specs or [VMEM] * len(args)) + [SMEM] * len(scalars),
        out_specs=out_specs or [VMEM] * len(outs),
        scratch_shapes=list(scratch),
        compiler_params=PARAMS,
        cost_estimate=pl.CostEstimate(flops=flops, bytes_accessed=size, transcendentals=0),
        name=name,
        **more,
    )(*args, *scalars)


def in_hbm(x):
    return pltpu.with_memory_space_constraint(x, pltpu.HBM)


def hbm(dims):
    return pltpu.HBM(dims, F32)


def pack(adjoint, state):
    (packed,) = call(
        pack_kernel,
        [hbm(PACKED_SHAPE)],
        [in_hbm(adjoint), in_hbm(state)],
        specs=[ANY, ANY],
        out_specs=[ANY],
        scratch=[room((2, *PLAIN_SHAPE)), room(PACKED_SHAPE), copies(16)],
        name="pack_blocks",
    )
    return packed


def regroup(x):
    return lax.all_to_all(x, "row", 0, 0, axis_index_groups=GROUPS, tiled=True)


def earlier(x):
    return lax.ppermute(x, "seg", [(i + 1, i) for i in range(7)])


def exchange(slabs, perms):
    arrived = [None] * len(perms)
    for at in (1, 2, 3, 0, 4):
        arrived[at] = lax.ppermute(slabs[at], "row", perms[at])
    return arrived


def body(
    terminal_adjoint,
    midpoint_state,
    controls,
    detuning,
    anharmonicity,
    decay_rate,
    dephasing,
    cross_kerr,
):
    amp = controls[0]
    dec = decay_rate[None]
    roots = jnp.asarray(ROOTS)[None]
    full = (amp, detuning[None], anharmonicity[None], dec, dephasing[None], cross_kerr[None], roots)
    few = (amp, dec, roots)
    terminal = terminal_adjoint[0]
    both = regroup(pack(terminal, midpoint_state[0, 0]))
    base = both.reshape(2 * UNITS, 2, ROWS, WIDTH)
    slabs = call(slab_kernel, SLAB_SHAPES, [base], name="slabs")
    current = base
    for n in range(3):
        scale = STEP if n == 2 else 0.5 * STEP
        halos = exchange(slabs, (PERM_I0, PERM_J1, PERM_J0, PERM_I2, PERM_CORNER))
        part, *middle = call(
            lambda *refs, n=n, scale=scale: local_kernel(scale, n, *refs),
            [UNIT_SHAPE] + [hbm(UNIT_SHAPE)] * (n == 2),
            [current, base],
            full,
            flops=30 << 20,
            size=6 << 20,
            out_specs=[VMEM] + [ANY] * (n == 2),
            scratch=[copies(1)] if n == 2 else [],
            name="local_terms",
        )
        if n < 2:
            current, *slabs = call(
                lambda *refs, scale=scale: edge_kernel(scale, False, *refs),
                [UNIT_SHAPE, *SLAB_SHAPES],
                [part, *halos],
                few,
                flops=5 << 20,
                size=8 << 20,
                name="edge_terms",
            )
    final, rest = call(
        lambda *refs: edge_kernel(STEP, True, *refs),
        [hbm(BLOCKS_SHAPE), hbm(REST_SHAPE)],
        [part, *halos],
        few,
        flops=5 << 20,
        size=6 << 20,
        out_specs=[ANY, ANY],
        scratch=[room(BLOCKS_SHAPE), copies(8)],
        name="edge_terms",
    )
    here = regroup(final)
    rest_next = earlier(rest)
    (grad,) = call(
        gradient_kernel,
        [(8, WIDTH)],
        [in_hbm(x) for x in (*middle, both, *halos[:4])],
        (roots,),
        flops=30 << 20,
        size=6 << 20,
        specs=[ANY] * 6,
        scratch=[room(UNIT_SHAPE), room((8, 4, 2, ROWS, WIDTH)), *map(room, SLAB_SHAPES[:4]), copies(6)],
        name="gradient",
    )
    grad = grad + lax.ppermute(grad, "row", PERM_I0)
    (joined,) = call(
        join_kernel,
        [hbm(JOINED_SHAPE)],
        [rest_next, grad],
        out_specs=[ANY],
        scratch=[copies(9)],
        name="join_blocks",
    )
    here, joined = lax.optimization_barrier((here, joined))
    rest_here = regroup(joined)
    (most,) = call(most_kernel, [MOST_SHAPE], [here], name="most_blocks")
    most_next = earlier(most)
    (start,) = call(
        start_kernel,
        [hbm(PLAIN_SHAPE)],
        [here],
        specs=[ANY],
        out_specs=[ANY],
        scratch=[room(BLOCKS_SHAPE), room(PLAIN_SHAPE), copies(8)],
        name="start_rows",
    )
    terminal = in_hbm(terminal)
    (defect,) = call(
        early_kernel,
        [hbm(PLAIN_SHAPE)],
        [most_next, terminal],
        specs=[ANY, ANY],
        out_specs=[ANY],
        scratch=[room(MOST_SHAPE), room(PLAIN_SHAPE), room(PLAIN_SHAPE), copies(3 * EARLY)],
        name="defect_early",
    )
    start, defect, rest_here = lax.optimization_barrier((start, defect, rest_here))
    defect, totals = call(
        late_kernel,
        [hbm(PLAIN_SHAPE), (1, 1, 4)],
        [defect, most_next, rest_here, terminal],
        specs=[ANY] * 4,
        out_specs=[ANY, VMEM],
        scratch=[room(MOST_SHAPE), room(JOINED_SHAPE), room(PLAIN_SHAPE), room(PLAIN_SHAPE), copies(7)],
        name="defect_late",
        input_output_aliases={0: 0},
    )
    return start[None], defect[None], totals


def solution(mesh):
    return jax.shard_map(
        body,
        mesh=mesh,
        in_specs=(
            P("seg", None, "row", None),
            P("seg", None, None, "row", None),
            P("seg", None, None),
            P(),
            P(),
            P(),
            P(),
            P(),
        ),
        out_specs=(P("seg", None, "row", None), P("seg", None, "row", None), P("seg", None, None)),
        check_vma=False,
    )
```

```python
import jax
import jax.numpy as jnp
import numpy as np
from jax import lax
from jax.experimental import pallas as pl
from jax.experimental.pallas import tpu as pltpu
from jax.sharding import PartitionSpec as P


ORDER = 2048
STEP = 0.01
UNITS = 32
ROWS = 16
LANES = 128
TILES = 4
WIDTH = TILES * LANES
F32 = jnp.float32

GROUPS = [
    [4 * y + z for y in (0, 1) for z in (0, 1, 3, 2)],
    [4 * y + z for y in (3, 2) for z in (2, 3, 1, 0)],
]
Y_OUTER = {0: 3, 3: 0, 1: 2, 2: 1}
Y_INNER = {0: 1, 1: 0, 2: 3, 3: 2}


def pairs_y(flip):
    return [(4 * y + z, 4 * flip[y] + z) for y in range(4) for z in range(4)]


def pairs_z(flip):
    return [(4 * y + z, 4 * y + flip[z]) for y in range(4) for z in range(4)]


PERM_I0 = pairs_y(Y_OUTER)
PERM_I2 = pairs_y(Y_INNER)
PERM_J0 = pairs_z(Y_OUTER)
PERM_J1 = pairs_z(Y_INNER)
PERM_CORNER = [(4 * y + z, 4 * Y_OUTER[y] + Y_OUTER[z]) for y in (0, 1) for z in (0, 1)]
ROOTS = np.sqrt(np.arange(16)).astype(np.float32)


class Place:
    def __init__(self):
        row = lax.axis_index("row")
        y = row >> 2
        z = row & 3
        self.upper = y >> 1
        self.gi2 = jnp.where((y == 1) | (y == 2), 1, 0)
        self.gj0 = z >> 1
        self.gj1 = jnp.where((z == 1) | (z == 2), 1, 0)


def unit_at(p, i1):
    odd = p & 1
    return ((p >> 1) << 4) + (((i1 >> 2) ^ (3 * odd)) << 2) + (i1 & 3)


def wide(unit):
    return unit + ((unit >> 2) << 2)


def iotas():
    lane = lax.broadcasted_iota(jnp.int32, (ROWS, LANES), 1)
    sub = lax.broadcasted_iota(jnp.int32, (ROWS, LANES), 0)
    return lane, sub


class Tables:
    def __init__(self, place):
        lane, sub = iotas()
        low1 = lane >> 5
        self.j1 = (low1 + 4 * place.gj1).astype(F32)
        self.j2 = ((lane >> 2) & 7).astype(F32)
        self.j3 = (lane & 3).astype(F32)
        low2 = sub >> 2
        self.i2 = (low2 + 4 * place.gi2).astype(F32)
        self.i3 = (sub & 3).astype(F32)
        self.c1p = jnp.where(low1 > 0, jnp.sqrt(self.j1), 0.0)
        self.c1m = jnp.where(low1 < 3, jnp.sqrt(self.j1 + 1.0), 0.0)
        self.c2p = jnp.sqrt(self.j2)
        self.c2m = jnp.where(self.j2 < 7.0, jnp.sqrt(self.j2 + 1.0), 0.0)
        self.c3p = jnp.sqrt(self.j3)
        self.c3m = jnp.where(self.j3 < 3.0, jnp.sqrt(self.j3 + 1.0), 0.0)
        self.r2p = jnp.where(low2 > 0, jnp.sqrt(self.i2), 0.0)
        self.r2m = jnp.where(low2 < 3, jnp.sqrt(self.i2 + 1.0), 0.0)
        self.r3p = jnp.sqrt(self.i3)
        self.r3m = jnp.where(self.i3 < 3.0, jnp.sqrt(self.i3 + 1.0), 0.0)
        edge1 = jnp.where(place.gj1 == 1, 0, 3)
        edge2 = jnp.where(place.gi2 == 1, 0, 3)
        self.edge1 = edge1
        self.at1 = (low1 == edge1).astype(F32)
        self.at2 = (low2 == edge2).astype(F32)


def drift(levels, detuning, anharmonicity, cross_kerr):
    total = 0.0
    for q in range(4):
        n = levels[q]
        total = total + detuning[q] * n - 0.5 * anharmonicity[q] * n * (n - 1.0)
    k = 0
    for a in range(4):
        for b in range(a + 1, 4):
            total = total - cross_kerr[k] * levels[a] * levels[b]
            k += 1
    return total


def decay_part(levels, decay, dephasing):
    total = 0.0
    for q in range(4):
        n = levels[q]
        total = total - 0.5 * decay[q] * n - 0.5 * dephasing[q] * n * n
    return total


def tile(ref, unit, c, t):
    return ref[unit, c, :, t * LANES : (t + 1) * LANES]


def level_of(place, p):
    return jnp.where(place.upper == 1, 7 - p, p)


def unit_neighbours(place, roots, p, i1, at=unit_at):
    up = place.upper == 1
    i0 = level_of(place, p)
    below = jnp.where(up, p + 1, p - 1)
    above = jnp.where(up, p - 1, p + 1)
    root_below = jnp.where((below >= 0) & (below <= 3), roots[0, i0], 0.0)
    root_above = jnp.where((above >= 0) & (above <= 3), roots[0, i0 + 1], 0.0)
    return (
        i0,
        (at(jnp.clip(below, 0, 3), i1), root_below),
        (at(jnp.clip(above, 0, 3), i1), root_above),
        (at(p, jnp.maximum(i1 - 1, 0)), roots[0, i1]),
        (at(p, jnp.minimum(i1 + 1, 7)), jnp.where(i1 < 7, roots[0, i1 + 1], 0.0)),
    )


def local_kernel(scale, n, *refs):
    z, base, *scalars, out = refs[:10]
    writes = []
    if n == 2:
        z_out, sems = refs[10:]
        writes = [pltpu.make_async_copy(z, z_out, sems.at[0])]
    start_all(writes)
    amp, det, anh, dec, dep, kerr, roots = scalars
    def at(p, i1):
        return unit_at(p, i1) if n else wide(unit_at(p, i1))

    place = Place()
    tb = Tables(place)
    detuning = [det[0, q] for q in range(4)]
    anharm = [anh[0, q] for q in range(4)]
    decay = [dec[0, q] for q in range(4)]
    dephasing = [dep[0, q] for q in range(4)]
    cross = [kerr[0, k] for k in range(6)]
    u = [amp[0, q] for q in range(4)]
    column_energy = []
    column_decay = []
    for t in range(TILES):
        j0 = (4 * place.gj0 + t).astype(F32)
        levels = [j0, tb.j1, tb.j2, tb.j3]
        column_energy.append(drift(levels, detuning, anharm, cross))
        column_decay.append(decay_part(levels, decay, dephasing))
    cross2 = dephasing[2] * tb.i2
    cross3 = dephasing[3] * tb.i3
    c1m, c2m, c3m = u[1] * tb.c1m, u[2] * tb.c2m, u[3] * tb.c3m
    c1p, c2p, c3p = u[1] * tb.c1p, u[2] * tb.c2p, u[3] * tb.c3p
    r2m, r3m = u[2] * tb.r2m, u[3] * tb.r3m
    r2p, r3p = u[2] * tb.r2p, u[3] * tb.r3p
    d2p, d3p = decay[2] * tb.r2p, decay[3] * tb.r3p

    def step(unit, carry):
        p = unit >> 3
        i1 = unit & 7
        here = unit_at(p, i1)
        mine = at(p, i1)
        i0, below, above, less, more = unit_neighbours(place, roots, p, i1, at)
        i0f = i0.astype(F32)
        i1f = i1.astype(F32)
        rows = [i0f, i1f, tb.i2, tb.i3]
        row_energy = drift(rows, detuning, anharm, cross)
        row_decay = decay_part(rows, decay, dephasing)
        d1p = (decay[1] * less[1]) * tb.c1p
        for t in range(TILES):
            j0 = 4 * place.gj0 + t
            root_left = roots[0, j0]
            root_right = roots[0, j0 + 1]
            comm = []
            sand = []
            values = []
            for c in range(2):
                m = tile(z, mine, c, t)
                values.append(m)
                turned2 = pltpu.roll(m, 4, 1)
                turned3 = pltpu.roll(m, 1, 1)
                row1 = tile(z, less[0], c, t)
                row0 = tile(z, below[0], c, t)
                k = (u[0] * below[1]) * row0 + (u[0] * above[1]) * tile(z, above[0], c, t)
                k = k + (u[1] * less[1]) * row1 + (u[1] * more[1]) * tile(z, more[0], c, t)
                if t > 0:
                    k = k - (u[0] * root_left) * tile(z, mine, c, t - 1)
                if t < TILES - 1:
                    k = k - (u[0] * root_right) * tile(z, mine, c, t + 1)
                k = k + r2p * pltpu.roll(m, 4, 0) + r2m * pltpu.roll(m, ROWS - 4, 0)
                k = k + r3p * pltpu.roll(m, 1, 0) + r3m * pltpu.roll(m, ROWS - 1, 0)
                k = k - c1p * pltpu.roll(m, 32, 1) - c1m * pltpu.roll(m, LANES - 32, 1)
                k = k - c2p * turned2 - c2m * pltpu.roll(m, LANES - 4, 1)
                k = k - c3p * turned3 - c3m * pltpu.roll(m, LANES - 1, 1)
                comm.append(k)
                s = (
                    d1p * pltpu.roll(row1, 32, 1)
                    + d2p * pltpu.roll(tb.c2p * turned2, 4, 0)
                    + d3p * pltpu.roll(tb.c3p * turned3, 1, 0)
                )
                if t > 0:
                    s = s + (decay[0] * below[1] * root_left) * tile(z, below[0], c, t - 1)
                sand.append(s)
            phase = row_energy - column_energy[t]
            damping = (
                row_decay
                + (column_decay[t] + (dephasing[0] * i0f) * j0.astype(F32))
                + (dephasing[1] * i1f) * tb.j1
                + cross2 * tb.j2
                + cross3 * tb.j3
            )
            x, y = values
            lanes = slice(t * LANES, (t + 1) * LANES)
            out[here, 0, :, lanes] = tile(base, wide(here), 0, t) + scale * (
                damping * x - phase * y - comm[1] + sand[0]
            )
            out[here, 1, :, lanes] = tile(base, wide(here), 1, t) + scale * (
                damping * y + phase * x + comm[0] + sand[1]
            )
        return carry

    lax.fori_loop(0, UNITS, step, 0, unroll=4)
    wait_all(writes)


def start_all(copies):
    for copy in copies:
        copy.start()


def wait_all(copies):
    for copy in copies:
        copy.wait()


def put_slabs(place, tb, p, pair, both, s_i0, s_j1, s_j0, s_i2, s_c):
    lane, _ = iotas()
    half = (lax.broadcasted_iota(jnp.int32, (8, LANES), 0) >> 2) == 1 - place.gi2
    block = lane >> 5
    gj0 = place.gj0 == 1
    gi2 = place.gi2 == 1
    for par in range(2):
        i1 = 2 * pair + par
        n = p * 8 + i1
        for c in range(2):
            tiles = both[par][c]
            if p == 3:
                for t in range(TILES):
                    s_i0[i1, c, :, t * LANES : (t + 1) * LANES] = tiles[t]
                s_c[i1, c] = tiles[TILES - 1]
            s_j0[2 * n + c] = jnp.where(gj0, tiles[0], tiles[TILES - 1])
            packed = tiles[0]
            for t in range(1, TILES):
                turned = pltpu.roll(tiles[t], 32 * t, 1)
                packed = jnp.where(block == ((tb.edge1 + t) & 3), turned, packed)
            s_j1[2 * n + c] = packed
    for c in range(2):
        for t in range(TILES):
            even, odd = both[0][c][t], both[1][c][t]
            stays = jnp.where(gi2, even[0:8], odd[8:16])
            moves = pltpu.roll(jnp.where(gi2, odd[0:8], even[8:16]), 4, 0)
            entry = ((p * 4 + pair) * 2 + c) * 2 + t // 2
            s_i2[entry, (t % 2) * 8 : (t % 2) * 8 + 8] = jnp.where(half, stays, moves)


def slab_kernel(z, s_i0, s_j1, s_j0, s_i2, s_c):
    place = Place()
    tb = Tables(place)
    for p in range(4):

        def step(pair, carry, p=p):
            both = [
                [[tile(z, wide(unit_at(p, 2 * pair + par)), c, t) for t in range(TILES)] for c in range(2)]
                for par in range(2)
            ]
            put_slabs(place, tb, p, pair, both, s_i0, s_j1, s_j0, s_i2, s_c)
            return carry

        lax.fori_loop(0, 4, step, 0, unroll=True)


def i2_halo(place, h_i2, p, pair, par, c, t):
    small = h_i2[((p * 4 + pair) * 2 + c) * 2 + t // 2, (t % 2) * 8 : (t % 2) * 8 + 8]
    turned = pltpu.roll(small, 4, 0)
    return jnp.where(place.gi2 == par, turned, small)


def edge_kernel(scale, last, *refs):
    part, h_i0, h_j1, h_j0, h_i2, h_c = refs[:6]
    if last:
        amp, dec, roots, out_all, out_rest, block, sems = refs[6:]
        later = 16 * MOST
    else:
        amp, dec, roots, out, *slabs = refs[6:]
    place = Place()
    tb = Tables(place)
    up = place.upper == 1
    upf = place.upper.astype(F32)
    gj0f = place.gj0.astype(F32)
    gj1f = place.gj1.astype(F32)
    gi2f = place.gi2.astype(F32)
    copies = []
    decay = [scale * dec[0, q] for q in range(4)]
    u = [scale * amp[0, q] for q in range(4)]
    s1_base = (decay[1] * 2.0 * gj1f) * tb.at1
    s2_base = ((decay[2] * 2.0 * gi2f) * tb.at2 * tb.c2p)[0:8]
    k1_mask = (-2.0 * u[1]) * tb.at1
    k2_mask = (2.0 * u[2]) * tb.at2

    def one(p, pair, par, kept):
        i0 = jnp.where(up, 7 - p, p)
        below = jnp.where(up, p + 1, p - 1)
        below_in = (below >= 0) & (below <= 3)
        below = jnp.clip(below, 0, 3)
        root_below = jnp.where(below_in, roots[0, i0], 0.0)
        i1 = 2 * pair + par
        here = unit_at(p, i1)
        n = p * 8 + i1
        s1_less = roots[0, i1] * s1_base
        n_less = p * 8 + jnp.maximum(i1 - 1, 0)
        new = [[], []]
        for t in range(TILES):
            j0 = 4 * place.gj0 + t
            lanes = slice(t * LANES, (t + 1) * LANES)
            turn = (32 * (2 * tb.edge1 - 3 - t)) & (LANES - 1)
            comm = []
            sand = []
            for c in range(2):
                across = i2_halo(place, h_i2, p, pair, par, c, t)
                own = pltpu.roll(h_j1[2 * n + c], turn, 1)
                if par == 0:
                    lower = pltpu.roll(h_j1[2 * n_less + c], turn, 1)
                else:
                    lower = kept[c, t]
                kept[c, t] = own
                k = k2_mask * jnp.concatenate([across, across], axis=0) + k1_mask * own
                first = s2_base * pltpu.roll(across, 4, 1)
                s = s1_less * lower
                s = jnp.concatenate([s[0:8] + first, s[8:16]], axis=0)
                if p == 3:
                    k = k + (2.0 * u[0]) * h_i0[i1, c, :, lanes]
                    if t > 0:
                        s = s + (decay[0] * 2.0 * upf * roots[0, j0]) * h_i0[
                            i1, c, :, (t - 1) * LANES : t * LANES
                        ]
                    else:
                        s = s + (decay[0] * 4.0 * upf * gj0f) * h_c[i1, c]
                if t == 0 or t == TILES - 1:
                    on = gj0f if t == 0 else 1.0 - gj0f
                    k = k - (2.0 * u[0] * on) * h_j0[2 * n + c]
                if t == 0:
                    s = s + (decay[0] * 2.0 * gj0f * root_below) * h_j0[2 * (below * 8 + i1) + c]
                comm.append(k)
                sand.append(s)
            new[0].append(tile(part, here, 0, t) + (sand[0] - comm[1]))
            new[1].append(tile(part, here, 1, t) + (sand[1] + comm[0]))
        return here, new

    for p in range(4):

        def step(pair, carry, p=p):
            both = []
            kept = {}
            for par in range(2):
                here, new = one(p, pair, par, kept)
                for c in range(2):
                    for t in range(TILES):
                        out[here, c, :, t * LANES : (t + 1) * LANES] = new[c][t]
                both.append(new)
            put_slabs(place, tb, p, pair, both, *slabs)
            return carry

        def last_step(h, carry, p=p):
            kept = {}
            for a in range(4):
                here, new = one(p, 2 * h + a // 2, a % 2, kept)
                for c in range(2):
                    for t in range(TILES):
                        lanes = slice(t * LANES, (t + 1) * LANES)
                        at = (2 * a + c) * ROWS
                        block[here >> 2, at : at + ROWS, lanes] = new[c][t]
            return carry

        if last:
            lax.fori_loop(0, 2, last_step, 0, unroll=True)
            slots = pl.ds(2 * p, 2)
            rows = pl.ds(later, 128 - later)
            copies.append(pltpu.make_async_copy(block.at[slots], out_all.at[slots], sems.at[p]))
            copies.append(pltpu.make_async_copy(block.at[slots, rows], out_rest.at[slots], sems.at[4 + p]))
            start_all(copies[-2:])
        else:
            lax.fori_loop(0, 4, step, 0, unroll=True)
    wait_all(copies)


def gradient_kernel(z_in, rho_in, i0_in, j1_in, j0_in, i2_in, roots, grad, z, rho, h_i0, h_j1, h_j0, h_i2, sems):
    reads = []
    for source, target in (
        (z_in, z),
        (rho_in.at[:, pl.ds(4, 4)], rho),
        (i0_in, h_i0),
        (j1_in, h_j1),
        (j0_in, h_j0),
        (i2_in, h_i2),
    ):
        reads.append(pltpu.make_async_copy(source, target, sems.at[len(reads)]))
    start_all(reads)
    place = Place()
    tb = Tables(place)
    gj0f = place.gj0.astype(F32)
    wait_all(reads)
    k1_mask = -2.0 * tb.at1
    k2_mask = 2.0 * tb.at2

    def half_step(n, par, acc):
        p = n >> 2
        pair = n & 3
        i1 = 2 * pair + par
        unit = p * 8 + i1
        here = unit_at(p, i1)
        _, below, above, less, more = unit_neighbours(place, roots, p, i1)
        outer = jnp.where(p == 3, 2.0, 0.0)
        for t in range(TILES):
            j0 = 4 * place.gj0 + t
            turn = (32 * (2 * tb.edge1 - 3 - t)) & (LANES - 1)
            for c in range(2):
                m = tile(z, here, c, t)
                k0 = below[1] * tile(z, below[0], c, t) + above[1] * tile(z, above[0], c, t)
                k0 = k0 + outer * h_i0[i1, c, :, t * LANES : (t + 1) * LANES]
                if t > 0:
                    k0 = k0 - roots[0, j0] * tile(z, here, c, t - 1)
                if t < TILES - 1:
                    k0 = k0 - roots[0, j0 + 1] * tile(z, here, c, t + 1)
                if t == 0 or t == TILES - 1:
                    on = gj0f if t == 0 else 1.0 - gj0f
                    k0 = k0 - (2.0 * on) * h_j0[2 * unit + c]
                k1 = less[1] * tile(z, less[0], c, t) + more[1] * tile(z, more[0], c, t)
                k1 = k1 - tb.c1p * pltpu.roll(m, 32, 1) - tb.c1m * pltpu.roll(m, LANES - 32, 1)
                k1 = k1 + k1_mask * pltpu.roll(h_j1[2 * unit + c], turn, 1)
                k2 = tb.r2p * pltpu.roll(m, 4, 0) + tb.r2m * pltpu.roll(m, ROWS - 4, 0)
                k2 = k2 - tb.c2p * pltpu.roll(m, 4, 1) - tb.c2m * pltpu.roll(m, LANES - 4, 1)
                across = i2_halo(place, h_i2, p, pair, par, c, t)
                k2 = k2 + k2_mask * jnp.concatenate([across, across], axis=0)
                k3 = tb.r3p * pltpu.roll(m, 1, 0) + tb.r3m * pltpu.roll(m, ROWS - 1, 0)
                k3 = k3 - tb.c3p * pltpu.roll(m, 1, 1) - tb.c3m * pltpu.roll(m, LANES - 1, 1)
                other = rho[here >> 2, here & 3, 1 - c, :, t * LANES : (t + 1) * LANES]
                if c == 1:
                    other = -other
                acc = [acc[q] + k * other for q, k in enumerate((k0, k1, k2, k3))]
        return acc

    def step(n, carry):
        acc = list(carry)
        for par in range(2):
            acc = half_step(n, par, acc)
        return tuple(acc)

    start = tuple(jnp.zeros((ROWS, LANES), F32) for _ in range(4))
    total = lax.fori_loop(0, UNITS // 2, step, start, unroll=2)
    for q in range(4):
        grad[:, q * LANES : (q + 1) * LANES] = total[q][0:8] + total[q][8:16]


def chunk_lanes(g, t):
    start = (g // 2) * 1024 + t * 256 + (g % 2) * 128
    return slice(start, start + LANES)


def slice_rows(a):
    return pl.ds(32 * a, 32)


def pack_kernel(adjoint, state, out, plain, block, sems):
    upper = lax.axis_index("row") >> 3
    reads = []
    for m, x in enumerate((adjoint, state)):
        for a in range(4):
            rows = slice_rows(a)
            reads.append(pltpu.make_async_copy(x.at[:, rows], plain.at[m, :, rows], sems.at[4 * m + a]))
    writes = [pltpu.make_async_copy(block.at[:, at], out.at[:, at], sems.at[8 + at]) for at in range(8)]
    start_all(reads)
    for at in range(8):
        m, a = at // 4, at % 4
        reads[at].wait()
        for gi2 in range(2):
            for g in range(4):
                k = 4 * gi2 + jnp.where(upper == 1, 3 - g, g)
                for c in range(2):
                    for t in range(TILES):
                        block[k, at, c, :, t * LANES : (t + 1) * LANES] = plain[
                            m, c, 32 * a + 16 * gi2 : 32 * a + 16 * gi2 + 16, chunk_lanes(g, t)
                        ]
        writes[at].start()
    wait_all(writes)


def join_kernel(blocks, grad, out, sems):
    rows = 16 * (8 - MOST)
    copies = [pltpu.make_async_copy(blocks, out.at[:, pl.ds(0, rows)], sems.at[8])]
    for k in range(8):
        copies.append(pltpu.make_async_copy(grad, out.at[k, pl.ds(rows, 8)], sems.at[k]))
    start_all(copies)
    wait_all(copies)


def undeal(upper, index, source, first, out, base=None):
    a, c = index // 2, index % 2
    for gi2 in range(2):
        rows = slice(32 * a + 16 * gi2, 32 * a + 16 * gi2 + 16)
        for g in range(4):
            k = 4 * gi2 + jnp.where(upper == 1, 3 - g, g)
            for t in range(TILES):
                lanes = chunk_lanes(g, t)
                value = source[k, first : first + 16, t * LANES : (t + 1) * LANES]
                if base is not None:
                    value = base[c, rows, lanes] - value
                out[c, rows, lanes] = value


def start_kernel(blocks, start, held, plain, sems):
    upper = lax.axis_index("row") >> 3
    reads = [
        pltpu.make_async_copy(blocks.at[:, pl.ds(32 * a, 32)], held.at[:, pl.ds(32 * a, 32)], sems.at[a])
        for a in range(4)
    ]
    writes = [
        pltpu.make_async_copy(plain.at[:, slice_rows(a)], start.at[:, slice_rows(a)], sems.at[4 + a])
        for a in range(4)
    ]
    start_all(reads)
    for a in range(4):
        reads[a].wait()
        for c in range(2):
            undeal(upper, 2 * a + c, held, 32 * a + 16 * c, plain)
        writes[a].start()
    wait_all(writes)


def early_kernel(most, base, defect, held, held_base, plain, sems):
    upper = lax.axis_index("row") >> 3
    reads = []
    writes = []
    for a in range(EARLY):
        rows = pl.ds(32 * a, 32)
        reads.append(pltpu.make_async_copy(most.at[:, rows], held.at[:, rows], sems.at[3 * a]))
        reads.append(pltpu.make_async_copy(base.at[:, rows], held_base.at[:, rows], sems.at[3 * a + 1]))
        writes.append(pltpu.make_async_copy(plain.at[:, rows], defect.at[:, rows], sems.at[3 * a + 2]))
    start_all(reads)
    for a in range(EARLY):
        wait_all(reads[2 * a : 2 * a + 2])
        for c in range(2):
            index = 2 * a + c
            undeal(upper, index, held, 16 * index, plain, held_base)
        writes[a].start()
    wait_all(writes)


def late_kernel(partial, most, rest, base, defect, total, held_most, held_rest, held_base, plain, sems):
    del partial
    upper = lax.axis_index("row") >> 3
    rows = 16 * (8 - MOST)
    first = 32 * EARLY
    reads = [
        pltpu.make_async_copy(rest, held_rest, sems.at[0]),
        pltpu.make_async_copy(
            base.at[:, pl.ds(first, 128 - first)], held_base.at[:, pl.ds(first, 128 - first)], sems.at[1]
        ),
        pltpu.make_async_copy(
            most.at[:, pl.ds(first, 16 * MOST - first)], held_most.at[:, pl.ds(first, 16 * MOST - first)], sems.at[2]
        ),
    ]
    order = range(3, EARLY - 1, -1)
    writes = [
        pltpu.make_async_copy(plain.at[:, slice_rows(a)], defect.at[:, slice_rows(a)], sems.at[3 + a])
        for a in order
    ]
    start_all(reads)
    wait_all(reads[:2])
    for at, a in enumerate(order):
        if at == 1:
            reads[2].wait()
        for c in range(2):
            index = 2 * a + c
            if index < MOST:
                undeal(upper, index, held_most, 16 * index, plain, held_base)
            else:
                undeal(upper, index, held_rest, 16 * (index - MOST), plain, held_base)
        writes[at].start()
    lane = lax.broadcasted_iota(jnp.int32, (1, 1, 4), 2)
    sums = jnp.zeros((1, 1, 4), F32)
    for q in range(4):
        part = held_rest[0, rows : rows + 8, q * LANES : (q + 1) * LANES]
        for k in range(1, 8):
            part = part + held_rest[k, rows : rows + 8, q * LANES : (q + 1) * LANES]
        sums = jnp.where(lane == q, jnp.sum(part) / ORDER, sums)
    total[...] = sums
    wait_all(writes)


def most_kernel(blocks, out):
    for k in range(8):
        out[k] = blocks[k, 0 : 16 * MOST]


VMEM = pl.BlockSpec(memory_space=pltpu.VMEM)
SMEM = pl.BlockSpec(memory_space=pltpu.SMEM)
ANY = pl.BlockSpec(memory_space=pl.ANY)
PARAMS = pltpu.CompilerParams(vmem_limit_bytes=16 * 1024 * 1024)
MOST = 5
EARLY = MOST // 2
UNIT_SHAPE = (UNITS, 2, ROWS, WIDTH)
PACKED_SHAPE = (8, 8, 2, ROWS, WIDTH)
PLAIN_SHAPE = (2, 128, ORDER)
BLOCKS_SHAPE = (8, 128, WIDTH)
MOST_SHAPE = (8, 16 * MOST, WIDTH)
REST_SHAPE = (8, 16 * (8 - MOST), WIDTH)
JOINED_SHAPE = (8, 16 * (8 - MOST) + 8, WIDTH)


SLAB_SHAPES = [(8, 2, ROWS, WIDTH)] + [(64, ROWS, LANES)] * 3 + [(8, 2, ROWS, LANES)]


def shape(dims):
    return jax.ShapeDtypeStruct(dims, F32)


def copies(count):
    return pltpu.SemaphoreType.DMA((count,))


def room(dims):
    return pltpu.VMEM(dims, F32)


def call(kernel, outs, args, scalars=(), flops=0, size=4 << 20, scratch=(), name=None, specs=None, out_specs=None, **more):
    out_shape = [shape(s) if isinstance(s, tuple) else s for s in outs]
    return pl.pallas_call(
        kernel,
        out_shape=out_shape,
        in_specs=(specs or [VMEM] * len(args)) + [SMEM] * len(scalars),
        out_specs=out_specs or [VMEM] * len(outs),
        scratch_shapes=list(scratch),
        compiler_params=PARAMS,
        cost_estimate=pl.CostEstimate(flops=flops, bytes_accessed=size, transcendentals=0),
        name=name,
        **more,
    )(*args, *scalars)


def in_hbm(x):
    return pltpu.with_memory_space_constraint(x, pltpu.HBM)


def hbm(dims):
    return pltpu.HBM(dims, F32)


def pack(adjoint, state):
    (packed,) = call(
        pack_kernel,
        [hbm(PACKED_SHAPE)],
        [in_hbm(adjoint), in_hbm(state)],
        specs=[ANY, ANY],
        out_specs=[ANY],
        scratch=[room((2, *PLAIN_SHAPE)), room(PACKED_SHAPE), copies(16)],
        name="pack_blocks",
    )
    return packed


def regroup(x):
    return lax.all_to_all(x, "row", 0, 0, axis_index_groups=GROUPS, tiled=True)


def earlier(x):
    return lax.ppermute(x, "seg", [(i + 1, i) for i in range(7)])


def exchange(slabs, perms):
    return [lax.ppermute(s, "row", perm) for s, perm in zip(slabs, perms)]


def body(
    terminal_adjoint,
    midpoint_state,
    controls,
    detuning,
    anharmonicity,
    decay_rate,
    dephasing,
    cross_kerr,
):
    amp = controls[0]
    dec = decay_rate[None]
    roots = jnp.asarray(ROOTS)[None]
    full = (amp, detuning[None], anharmonicity[None], dec, dephasing[None], cross_kerr[None], roots)
    few = (amp, dec, roots)
    terminal = terminal_adjoint[0]
    both = regroup(pack(terminal, midpoint_state[0, 0]))
    base = both.reshape(2 * UNITS, 2, ROWS, WIDTH)
    slabs = call(slab_kernel, SLAB_SHAPES, [base], name="slabs")
    current = base
    for n in range(3):
        scale = STEP if n == 2 else 0.5 * STEP
        halos = exchange(slabs, (PERM_I0, PERM_J1, PERM_J0, PERM_I2, PERM_CORNER))
        part, *middle = call(
            lambda *refs, n=n, scale=scale: local_kernel(scale, n, *refs),
            [UNIT_SHAPE] + [hbm(UNIT_SHAPE)] * (n == 2),
            [current, base],
            full,
            flops=30 << 20,
            size=6 << 20,
            out_specs=[VMEM] + [ANY] * (n == 2),
            scratch=[copies(1)] if n == 2 else [],
            name="local_terms",
        )
        if n < 2:
            current, *slabs = call(
                lambda *refs, scale=scale: edge_kernel(scale, False, *refs),
                [UNIT_SHAPE, *SLAB_SHAPES],
                [part, *halos],
                few,
                flops=5 << 20,
                size=8 << 20,
                name="edge_terms",
            )
    final, rest = call(
        lambda *refs: edge_kernel(STEP, True, *refs),
        [hbm(BLOCKS_SHAPE), hbm(REST_SHAPE)],
        [part, *halos],
        few,
        flops=5 << 20,
        size=6 << 20,
        out_specs=[ANY, ANY],
        scratch=[room(BLOCKS_SHAPE), copies(8)],
        name="edge_terms",
    )
    here = regroup(final)
    rest_next = earlier(rest)
    (grad,) = call(
        gradient_kernel,
        [(8, WIDTH)],
        [in_hbm(x) for x in (*middle, both, *halos[:4])],
        (roots,),
        flops=30 << 20,
        size=6 << 20,
        specs=[ANY] * 6,
        scratch=[room(UNIT_SHAPE), room((8, 4, 2, ROWS, WIDTH)), *map(room, SLAB_SHAPES[:4]), copies(6)],
        name="gradient",
    )
    grad = grad + lax.ppermute(grad, "row", PERM_I0)
    (joined,) = call(
        join_kernel,
        [hbm(JOINED_SHAPE)],
        [rest_next, grad],
        out_specs=[ANY],
        scratch=[copies(9)],
        name="join_blocks",
    )
    here, joined = lax.optimization_barrier((here, joined))
    rest_here = regroup(joined)
    (most,) = call(most_kernel, [MOST_SHAPE], [here], name="most_blocks")
    most_next = earlier(most)
    (start,) = call(
        start_kernel,
        [hbm(PLAIN_SHAPE)],
        [here],
        specs=[ANY],
        out_specs=[ANY],
        scratch=[room(BLOCKS_SHAPE), room(PLAIN_SHAPE), copies(8)],
        name="start_rows",
    )
    terminal = in_hbm(terminal)
    (defect,) = call(
        early_kernel,
        [hbm(PLAIN_SHAPE)],
        [most_next, terminal],
        specs=[ANY, ANY],
        out_specs=[ANY],
        scratch=[room(MOST_SHAPE), room(PLAIN_SHAPE), room(PLAIN_SHAPE), copies(3 * EARLY)],
        name="defect_early",
    )
    start, defect, rest_here = lax.optimization_barrier((start, defect, rest_here))
    defect, totals = call(
        late_kernel,
        [hbm(PLAIN_SHAPE), (1, 1, 4)],
        [defect, most_next, rest_here, terminal],
        specs=[ANY] * 4,
        out_specs=[ANY, VMEM],
        scratch=[room(MOST_SHAPE), room(JOINED_SHAPE), room(PLAIN_SHAPE), room(PLAIN_SHAPE), copies(7)],
        name="defect_late",
        input_output_aliases={0: 0},
    )
    return start[None], defect[None], totals


def solution(mesh):
    return jax.shard_map(
        body,
        mesh=mesh,
        in_specs=(
            P("seg", None, "row", None),
            P("seg", None, None, "row", None),
            P("seg", None, None),
            P(),
            P(),
            P(),
            P(),
            P(),
        ),
        out_specs=(P("seg", None, "row", None), P("seg", None, "row", None), P("seg", None, None)),
        check_vma=False,
    )
```
